128 devices in a mesh: row: 16 (over y, z_lo, core), col: 8 (over z_hi, x).
Axes of the slice: x: 4, y: 4, z: 4 (z_hi: 2, z_lo: 2; z = z_hi * 2 + z_lo), core: 2. Of those that a mesh axis runs over, the one named last changes fastest.
Arguments:
- blocks: bfloat16 [49152, 128, 128], P(('row', 'col')), may hold values from -0.109375 to 0.109375
- block_row: int32 [49152], P(('row', 'col')), may hold values from 0 to 127, as said below
- block_col: int32 [49152], P(('row', 'col')), may hold values from 0 to 255
- random_cols: bfloat16 [8, 16, 2048, 256], P('col', 'row'), may hold values from -6 to 6
- leaf_perm: int32 [128, 2048], P(('row', 'col')), may hold values from 0 to 2047, each once within a row
- parent_perm: int32 [64, 256], replicated, may hold values from 0 to 255, each once within a row
Outputs:
- leaf_basis: float32 [262144, 128], P(('row', 'col'))
- parent_basis: float32 [16384, 128], P(('row', 'col'))
The draws below stay inside these ranges and needn't reach their ends.
Inputs may be any that keep to these rules, and one draw needn't show every extreme that they name: `block_row`: each device's 384 entries name every block row 0 to 127 at least once.
All inputs are finite; a program needn't handle non-finite values.
Results may differ from the reference program's by a relative error of at most 0.027.
Values may be sent and summed in bfloat16 or wider, within the bound.
A program may use at most 192 MiB of HBM per device.

```python
import jax
import jax.numpy as jnp
from jax import lax

BLK = 128
S = 256
RANK = 128
LEAF = 2048
NB_DEV = 384
N = 262144
BR = 128
BC = 256
PARENTS = 64
N_ROW = 16
N_COL = 8


def draw_block_row(key, part):
    key = jax.random.fold_in(key, 11)

    def one_device(dev_key):
        first_key, second_key, third_key = jax.random.split(dev_key, 3)
        cover = jax.random.permutation(first_key, BR).astype(jnp.int32)
        extra = jax.random.randint(second_key, (NB_DEV - BR,), 0, BR).astype(jnp.int32)
        joined = jnp.concatenate([cover, extra])
        order = jax.random.permutation(third_key, NB_DEV)
        return joined[order]
    dev_keys = jax.random.split(key, N_ROW * N_COL)
    return jax.vmap(one_device)(dev_keys).reshape(-1).astype(jnp.int32)


def touch_ends(result, own_key, smallest, largest):
    longest = result.shape.index(max(result.shape))
    spots = []
    for shift in (0, 1):
        where = [jax.random.randint(jax.random.fold_in(own_key, axis), (), 0, length) for axis, length in enumerate(result.shape)]
        where[longest] = (where[longest] + shift) % result.shape[longest]
        spots.append(tuple(where))
    return result.at[spots[0]].set(smallest).at[spots[1]].set(largest)


def shard_levels(key, extent, pieces, smallest, top_value):
    factor_of, own = 1.0, jax.random.fold_in(key, 6)
    for axis_at, parts in pieces:
        steps = jnp.exp(jax.random.uniform(jax.random.fold_in(own, axis_at), (parts,), jnp.float32, smallest / len(pieces), top_value / len(pieces)))
        factor_of = factor_of * jnp.repeat(steps, extent[axis_at] // parts).reshape([-1 if axis == axis_at else 1 for axis in range(len(extent))])
    return factor_of


def normal_values(rng, extent, deviation, limit, cuts=(), kind=jnp.bfloat16):
    drawn = jax.random.normal(rng, extent, jnp.float32) * deviation
    if len(cuts) > 0:
        drawn = shard_levels(rng, extent, cuts, -0.22, 0.18) * drawn
    return jnp.clip(drawn, min=-limit, max=limit).astype(kind)


def setup_inputs(seed: int = 0) -> dict:
    key_list = jax.random.split(jax.random.key(seed), 7)
    blocks = normal_values(key_list[0], (N_ROW * N_COL * NB_DEV, BLK, BLK), (BLK * NB_DEV * N_COL // BR) ** -0.5, 0.109375, ((0, 128),))
    block_row = draw_block_row(jax.random.fold_in(key_list[6], 71), 0)
    block_col = touch_ends(jax.random.randint(key_list[2], (N_ROW * N_COL * NB_DEV,), 0, BC), jax.random.fold_in(key_list[2], 1), 0, BC - 1).astype(jnp.int32)
    random_cols = normal_values(key_list[3], (N_COL, N_ROW, LEAF, S), 1.0, 6.0, ((0, 8), (1, 16)))
    leaf_perm = jax.vmap(lambda own: jax.random.permutation(own, LEAF))(jax.random.split(key_list[4], (N_ROW * N_COL))).reshape((N_ROW * N_COL, LEAF)).astype(jnp.int32)
    parent_perm = jax.vmap(lambda own: jax.random.permutation(own, 2 * RANK))(jax.random.split(key_list[5], PARENTS)).reshape((PARENTS, 2 * RANK)).astype(jnp.int32)
    return {"blocks": blocks, "block_row": block_row, "block_col": block_col, "random_cols": random_cols, "leaf_perm": leaf_perm, "parent_perm": parent_perm}


HI = lax.Precision.HIGHEST

def interp(full, skel):
    gram = jnp.dot(skel.astype(jnp.float32), skel.T.astype(jnp.float32), precision=HI, preferred_element_type=jnp.float32)
    cross = jnp.dot(full.astype(jnp.float32), skel.T.astype(jnp.float32), precision=HI, preferred_element_type=jnp.float32)
    factor = jnp.linalg.cholesky(gram)
    first = lax.linalg.triangular_solve(factor, cross, left_side=False, lower=True, transpose_a=True)
    return lax.linalg.triangular_solve(factor, first, left_side=False, lower=True, transpose_a=False)

def reference(blocks, block_row, block_col, random_cols, leaf_perm, parent_perm):
    ndev = N_ROW * N_COL
    rand_blocks = random_cols.reshape(N // BLK, BLK, S)
    blk_dev = blocks.reshape(ndev, NB_DEV, BLK, BLK)
    rows_dev = block_row.reshape(ndev, NB_DEV)
    cols_dev = block_col.reshape(ndev, NB_DEV)

    def step(total, dev):
        rindex = dev // N_COL
        cindex = dev % N_COL
        mats = blk_dev[dev].astype(jnp.float32)
        picked = rand_blocks[cindex * BC + cols_dev[dev]].astype(jnp.float32)
        prods = jnp.einsum('gij,gjs->gis', mats, picked, precision=HI)
        part = jax.ops.segment_sum(prods, rows_dev[dev], num_segments=BR)
        part = lax.optimization_barrier(part.astype(jnp.bfloat16)).astype(jnp.float32)
        old = lax.dynamic_index_in_dim(total, rindex, 0, keepdims=False)
        total = lax.dynamic_update_index_in_dim(total, old + part, rindex, 0)
        return (total, None)
    total0 = jnp.zeros((N_ROW, BR, BLK, S), jnp.float32)
    total, _ = lax.scan(step, total0, jnp.arange(ndev, dtype=jnp.int32))
    leaves = total.reshape(ndev, LEAF, S)

    def leaf_fn(rows, perm):
        skel = rows[perm[:RANK]]
        return (interp(rows, skel), skel)
    leaf_basis, skels = jax.vmap(leaf_fn)(leaves, leaf_perm)
    stacked = skels.reshape(ndev // 2, 2 * RANK, S)

    def parent_fn(rows, perm):
        return interp(rows, rows[perm[:RANK]])
    parent_basis = jax.vmap(parent_fn)(stacked, parent_perm)
    return (leaf_basis.reshape(N, RANK), parent_basis.reshape(ndev * RANK, RANK))
```

```python
import functools

import jax
import jax.numpy as jnp
from jax import lax
from jax.experimental import pallas as pl
from jax.experimental.pallas import tpu as pltpu
from jax.sharding import PartitionSpec as P

HI = lax.Precision.HIGHEST
VMEM = pl.BlockSpec(memory_space=pltpu.VMEM)
SMEM = pl.BlockSpec(memory_space=pltpu.SMEM)
F32 = jnp.float32
BF16 = jnp.bfloat16


def schedule(rows, cols, nrows):
    count = rows.shape[0]
    steps = (count + nrows) // 2
    k = jnp.arange(count, dtype=jnp.int32)
    i = jnp.arange(nrows, dtype=jnp.int32)
    q = jnp.arange(steps, dtype=jnp.int32)
    same = (rows[None, :] == rows[:, None]) & (k[None, :] < k[:, None])
    within = jnp.sum(same.astype(jnp.int32), axis=1)
    held = jnp.sum((rows[None, :] == i[:, None]).astype(jnp.int32), axis=1)
    pairs = (held + 1) // 2
    before = jnp.sum(jnp.where(i[None, :] < i[:, None], pairs[None, :], 0), axis=1)
    base = jnp.sum(jnp.where(i[None, :] < rows[:, None], pairs[None, :], 0), axis=1)
    place = 2 * base + within
    t = jnp.arange(2 * steps, dtype=jnp.int32)
    code = (k + 1) * 65536 + cols
    slots = jnp.sum(jnp.where(t[:, None] == place[None, :], code[None, :], 0), axis=1)
    row = jnp.minimum(jnp.sum(((before + pairs)[None, :] <= q[:, None]).astype(jnp.int32), axis=1), nrows - 1)
    first = jnp.sum((before[None, :] == q[:, None]).astype(jnp.int32), axis=1)
    total = jnp.sum(pairs).reshape(1)
    return slots, row * 2 + first, total


UNROLL = 4


def spmm_kernel(slots, steps, total, blocks, rand, out, acc):
    acc[...] = jnp.zeros_like(acc)

    def pair(q):
        mats, rights = [], []
        for s in range(2):
            code = slots[2 * q + s]
            k = jnp.maximum(lax.shift_right_logical(code, 16) - 1, 0)
            col = jnp.bitwise_and(code, 65535)
            mat = blocks[k]
            mats.append(jnp.where(code > 0, mat, jnp.zeros_like(mat)))
            rights.append(rand[col])
        return jnp.dot(
            jnp.concatenate(mats, axis=1),
            jnp.concatenate(rights, axis=0),
            preferred_element_type=F32,
        )

    def body(g, carry):
        prods = [pair(g * UNROLL + u) for u in range(UNROLL)]
        for u in range(UNROLL):
            info = steps[g * UNROLL + u]
            keep = (1 - jnp.bitwise_and(info, 1)).astype(F32)
            value = acc[...] * keep + prods[u]
            acc[...] = value
            out[lax.shift_right_logical(info, 1)] = value.astype(BF16)
        return carry

    lax.fori_loop(0, (total[0] + UNROLL - 1) // UNROLL, body, 0)


def spmm(slots, steps, total, blocks, rand, nrows):
    size, width = blocks.shape[1], rand.shape[2]
    return pl.pallas_call(
        spmm_kernel,
        name="spmm",
        out_shape=jax.ShapeDtypeStruct((nrows, size, width), BF16),
        in_specs=[SMEM, SMEM, SMEM, VMEM, VMEM],
        out_specs=VMEM,
        scratch_shapes=[pltpu.VMEM((size, width), F32)],
        compiler_params=pltpu.CompilerParams(vmem_limit_bytes=48 << 20),
    )(slots, steps, total, blocks, rand)


def pick_kernel(perm, full, out):
    lanes = lax.broadcasted_iota(jnp.int32, (perm.shape[0], full.shape[0]), 1)
    hot = jnp.where(lanes == perm[...], 1.0, 0.0).astype(BF16)
    out[...] = jnp.dot(hot, full[...], preferred_element_type=F32).astype(BF16)


def dot_t(a, b):
    return lax.dot_general(a, b, (((1,), (1,)), ((), ())), preferred_element_type=F32)


def inverses(mats):
    n = mats[0].shape[0]
    lane = lax.broadcasted_iota(jnp.int32, (n, n), 1)
    sub = lax.broadcasted_iota(jnp.int32, (n, n), 0)
    lane1 = lax.broadcasted_iota(jnp.int32, (1, n), 1)
    sub1 = lax.broadcasted_iota(jnp.int32, (n, 1), 0)
    for k in range(n):
        cross = (lane == k) | (sub == k)
        done = []
        for a in mats:
            inv = 1.0 / a[k : k + 1, k : k + 1]
            row = jnp.where(lane1 == k, -inv, a[k : k + 1, :] * inv)
            col = jnp.where(sub1 == k, -1.0, a[:, k : k + 1])
            done.append(jnp.where(cross, 0.0, a) - col * row)
        mats = done
    return [-a for a in mats]


def solve_kernel(perm, full, own, low, high, basis, parent):
    both = jnp.concatenate([low[...], high[...]], axis=0)
    lanes = lax.broadcasted_iota(jnp.int32, (perm.shape[0], both.shape[0]), 1)
    hot = jnp.where(lanes == perm[...], 1.0, 0.0).astype(BF16)
    skel = jnp.dot(hot, both, preferred_element_type=F32).astype(BF16)
    mine = own[...]
    inv_leaf, inv_parent = inverses([dot_t(mine, mine), dot_t(skel, skel)])
    parent[...] = jnp.dot(dot_t(mine, skel), inv_parent, precision=HI, preferred_element_type=F32)
    tile = 512

    def body(i, carry):
        at = pl.ds(pl.multiple_of(i * tile, tile), tile)
        cross = dot_t(full[at, :], mine)
        basis[at, :] = jnp.dot(cross, inv_leaf, precision=HI, preferred_element_type=F32)
        return carry

    lax.fori_loop(0, full.shape[0] // tile, body, 0)


def local(blocks, block_row, block_col, random_cols, leaf_perm, parent_perm):
    n_col = lax.axis_size("col")
    leaf_rows, width = random_cols.shape[2:]
    size = blocks.shape[1]
    nrows = leaf_rows * n_col // size
    rank = parent_perm.shape[1] // 2
    slots, steps, total = schedule(block_row, block_col, nrows)
    gathered = lax.all_gather(random_cols.reshape(leaf_rows, width), "row", axis=0, tiled=True)
    partial_value = spmm(slots, steps, total, blocks, gathered.reshape(-1, size, width), nrows)
    leaf = lax.psum_scatter(
        partial_value.reshape(nrows * size, width), "col", scatter_dimension=0, tiled=True
    )
    skel = pl.pallas_call(
        pick_kernel,
        name="pick",
        out_shape=jax.ShapeDtypeStruct((rank, width), BF16),
        in_specs=[VMEM, VMEM],
        out_specs=VMEM,
        compiler_params=pltpu.CompilerParams(vmem_limit_bytes=32 << 20),
    )(leaf_perm[0, :rank].reshape(rank, 1), leaf)
    cindex = lax.axis_index("col")
    other = lax.ppermute(skel, "col", [(s, s ^ 1) for s in range(n_col)])
    parity = cindex % 2
    low = jnp.where(parity == 0, skel, other)
    high = jnp.where(parity == 0, other, skel)
    device = lax.axis_index("row") * n_col + cindex
    perm = lax.dynamic_index_in_dim(parent_perm, device // 2, 0, keepdims=False)[:rank]
    return pl.pallas_call(
        solve_kernel,
        name="solve",
        out_shape=(
            jax.ShapeDtypeStruct((leaf_rows, rank), F32),
            jax.ShapeDtypeStruct((rank, rank), F32),
        ),
        in_specs=[VMEM] * 5,
        out_specs=(VMEM, VMEM),
        compiler_params=pltpu.CompilerParams(vmem_limit_bytes=32 << 20),
    )(perm.reshape(rank, 1), leaf, skel, low, high)


def solution(mesh):
    in_specs = (
        P(("row", "col"), None, None),
        P(("row", "col")),
        P(("row", "col")),
        P("col", "row", None, None),
        P(("row", "col"), None),
        P(),
    )
    out_specs = (P(("row", "col"), None), P(("row", "col"), None))
    return jax.shard_map(local, mesh=mesh, in_specs=in_specs, out_specs=out_specs, check_vma=False)
```

```python
import functools

import jax
import jax.numpy as jnp
from jax import lax
from jax.experimental import pallas as pl
from jax.experimental.pallas import tpu as pltpu
from jax.sharding import PartitionSpec as P

HI = lax.Precision.HIGHEST
VMEM = pl.BlockSpec(memory_space=pltpu.VMEM)
SMEM = pl.BlockSpec(memory_space=pltpu.SMEM)
HBM = pl.BlockSpec(memory_space=pltpu.HBM)
F32 = jnp.float32
BF16 = jnp.bfloat16


def schedule(rows, cols, nrows):
    count = rows.shape[0]
    steps = (count + nrows) // 2
    k = jnp.arange(count, dtype=jnp.int32)
    i = jnp.arange(nrows, dtype=jnp.int32)
    q = jnp.arange(steps, dtype=jnp.int32)
    same = (rows[None, :] == rows[:, None]) & (k[None, :] < k[:, None])
    within = jnp.sum(same.astype(jnp.int32), axis=1)
    held = jnp.sum((rows[None, :] == i[:, None]).astype(jnp.int32), axis=1)
    pairs = (held + 1) // 2
    before = jnp.sum(jnp.where(i[None, :] < i[:, None], pairs[None, :], 0), axis=1)
    base = jnp.sum(jnp.where(i[None, :] < rows[:, None], pairs[None, :], 0), axis=1)
    place = 2 * base + within
    t = jnp.arange(2 * steps, dtype=jnp.int32)
    code = (k + 1) * 65536 + cols
    slots = jnp.sum(jnp.where(t[:, None] == place[None, :], code[None, :], 0), axis=1)
    row = jnp.minimum(jnp.sum(((before + pairs)[None, :] <= q[:, None]).astype(jnp.int32), axis=1), nrows - 1)
    first = jnp.sum((before[None, :] == q[:, None]).astype(jnp.int32), axis=1)
    total = jnp.sum(pairs).reshape(1)
    return slots, row * 2 + first, total


MESH = pl.DeviceIdType.MESH


OFFSETS = ((1, 2), (0, 2), (1, 1), (1, 3), (0, 1), (0, 3), (1, 0))


def col_peers():
    c = lax.axis_index("col")
    zh, x = c // 4, lax.rem(c, 4)
    return [lax.rem(zh + dz, 2) * 4 + lax.rem(x + dx, 4) for dz, dx in OFFSETS]


def gather_kernel(
    own, perm, out, perms, local_sem, send_sem, recv_sem, core_send, core_recv, perm_local, perm_send, perm_recv
):
    r = lax.axis_index("row")
    y, zl, co = r // 4, lax.rem(r // 2, 2), lax.rem(r, 2)
    size = own.shape[0]
    half = size // 2
    low = size * 7 // 16
    mid = low + (size - low) // 2

    def at(dy, dz, dc=0):
        return lax.rem(y + dy + 4, 4) * 4 + lax.rem(zl + dz, 2) * 2 + lax.rem(co + dc, 2)

    up, down, side, core = at(1, 0), at(-1, 0), at(0, 1), at(0, 0, 1)
    barrier = pltpu.get_barrier_semaphore()
    for peer in (up, down, side, core):
        pl.semaphore_signal(barrier, inc=1, device_id={"row": peer}, device_id_type=MESH)
    peers = col_peers()
    for j in peers:
        pl.semaphore_signal(barrier, inc=1, device_id={"col": j}, device_id_type=MESH)
    keep = pltpu.make_async_copy(own, out.at[pl.ds(pl.multiple_of(r * size, size), size)], local_sem)
    keep.start()
    keep_perm = pltpu.make_async_copy(perm, perms.at[lax.axis_index("col")], perm_local)
    keep_perm.start()
    pl.semaphore_wait(barrier, 4 + len(peers))

    def rows(source, first, last):
        return pl.ds(pl.multiple_of(source * size + first, 16), last - first)

    sent = []

    def send(source, first, last, target, slot, mine=False):
        dst = out.at[rows(source, first, last)]
        cp = pltpu.make_async_remote_copy(
            src_ref=own.at[pl.ds(first, last - first)] if mine else dst,
            dst_ref=dst,
            send_sem=send_sem.at[len(sent)],
            recv_sem=recv_sem.at[slot],
            device_id={"row": target},
            device_id_type=MESH,
        )
        cp.start()
        sent.append(cp)

    crossed = []

    def cross(source, first, last, mine=False):
        dst = out.at[rows(source, first, last)]
        cp = pltpu.make_async_remote_copy(
            src_ref=own if mine else dst,
            dst_ref=dst,
            send_sem=core_send.at[len(crossed)],
            recv_sem=core_recv.at[len(crossed)],
            device_id={"row": core},
            device_id_type=MESH,
        )
        cp.start()
        crossed.append(cp)

    def arrived(source, first, last, slot):
        dst = out.at[rows(source, first, last)]
        pltpu.make_async_remote_copy(
            src_ref=dst,
            dst_ref=dst,
            send_sem=send_sem.at[0],
            recv_sem=recv_sem.at[slot],
            device_id={"row": core},
            device_id_type=MESH,
        ).wait_recv()

    send(r, 0, half, up, 0, True)
    send(r, half, size, down, 2, True)
    send(r, low, size, side, 4, True)
    send(r, half, size, up, 1, True)
    send(r, 0, half, down, 3, True)
    send(r, 0, low, side, 5, True)
    cross(r, 0, size, True)
    orders = []
    for i, j in enumerate(peers):
        cp = pltpu.make_async_remote_copy(
            src_ref=perm,
            dst_ref=perms.at[lax.axis_index("col")],
            send_sem=perm_send.at[i],
            recv_sem=perm_recv.at[i],
            device_id={"col": j},
            device_id_type=MESH,
        )
        cp.start()
        orders.append(cp)

    prev, nxt, far = at(-1, 0), at(1, 0), at(2, 0)
    zown, zprev, znext, zfar = at(0, 1), at(-1, 1), at(1, 1), at(2, 1)

    arrived(prev, 0, half, 0)
    send(prev, 0, half, up, 6)
    send(prev, 0, low, side, 10)
    cross(prev, 0, half)
    arrived(nxt, half, size, 2)
    send(nxt, half, size, down, 7)
    cross(nxt, half, size)
    arrived(zown, low, size, 4)
    send(zown, low, size, up, 8)
    send(zown, low, size, down, 9)
    cross(zown, low, size)
    arrived(nxt, 0, half, 3)
    send(nxt, 0, low, side, 11)
    cross(nxt, 0, half)
    arrived(prev, half, size, 1)
    cross(prev, half, size)
    arrived(zown, 0, low, 5)
    cross(zown, 0, low)
    arrived(far, 0, half, 6)
    send(far, 0, low, side, 14)
    cross(far, 0, half)
    arrived(far, half, size, 7)
    cross(far, half, size)
    arrived(zprev, low, size, 8)
    send(zprev, low, mid, up, 12)
    cross(zprev, low, size)
    arrived(znext, low, size, 9)
    send(znext, mid, size, down, 13)
    cross(znext, low, size)
    arrived(zprev, 0, low, 10)
    cross(zprev, 0, low)
    arrived(znext, 0, low, 11)
    cross(znext, 0, low)
    arrived(zfar, low, mid, 12)
    cross(zfar, low, mid)
    arrived(zfar, mid, size, 13)
    cross(zfar, mid, size)
    arrived(zfar, 0, low, 14)
    cross(zfar, 0, low)
    keep.wait()
    keep_perm.wait()
    for cp in orders:
        cp.wait()
    for cp in sent:
        cp.wait_send()
    for cp in crossed:
        cp.wait()


def gather(own, perm):
    size, width = own.shape
    count, n_col = lax.axis_size("row"), lax.axis_size("col")
    return pl.pallas_call(
        gather_kernel,
        name="gather",
        out_shape=(
            jax.ShapeDtypeStruct((count * size, width), own.dtype),
            jax.ShapeDtypeStruct((n_col, *perm.shape), perm.dtype),
        ),
        in_specs=[HBM, HBM],
        out_specs=(HBM, HBM),
        scratch_shapes=[
            pltpu.SemaphoreType.DMA,
            pltpu.SemaphoreType.DMA((16,)),
            pltpu.SemaphoreType.DMA((15,)),
            pltpu.SemaphoreType.DMA((16,)),
            pltpu.SemaphoreType.DMA((16,)),
            pltpu.SemaphoreType.DMA,
            pltpu.SemaphoreType.DMA((n_col - 1,)),
            pltpu.SemaphoreType.DMA((n_col - 1,)),
        ],
        compiler_params=pltpu.CompilerParams(collective_id=0, has_side_effects=True),
    )(own, perm)


UNROLL = 4


def spmm_kernel(slots, steps, total, blocks, rand, out, acc):
    acc[...] = jnp.zeros_like(acc)

    def pair(q):
        mats, rights = [], []
        for s in range(2):
            code = slots[2 * q + s]
            k = jnp.maximum(lax.shift_right_logical(code, 16) - 1, 0)
            col = jnp.bitwise_and(code, 65535)
            mat = blocks[k]
            mats.append(jnp.where(code > 0, mat, jnp.zeros_like(mat)))
            rights.append(rand[col])
        return jnp.dot(
            jnp.concatenate(mats, axis=1),
            jnp.concatenate(rights, axis=0),
            preferred_element_type=F32,
        )

    def body(g, carry):
        prods = [pair(g * UNROLL + u) for u in range(UNROLL)]
        for u in range(UNROLL):
            info = steps[g * UNROLL + u]
            keep = (1 - jnp.bitwise_and(info, 1)).astype(F32)
            value = acc[...] * keep + prods[u]
            acc[...] = value
            out[lax.shift_right_logical(info, 1)] = value.astype(BF16)
        return carry

    lax.fori_loop(0, (total[0] + UNROLL - 1) // UNROLL, body, 0)


def spmm(slots, steps, total, blocks, rand, nrows):
    size, width = blocks.shape[1], rand.shape[2]
    return pl.pallas_call(
        spmm_kernel,
        name="spmm",
        out_shape=jax.ShapeDtypeStruct((nrows, size, width), BF16),
        in_specs=[SMEM, SMEM, SMEM, VMEM, VMEM],
        out_specs=VMEM,
        scratch_shapes=[pltpu.VMEM((size, width), F32)],
        compiler_params=pltpu.CompilerParams(vmem_limit_bytes=48 << 20),
    )(slots, steps, total, blocks, rand)


def dot_t(a, b):
    return lax.dot_general(a, b, (((1,), (1,)), ((), ())), preferred_element_type=F32)


def inverse_small(d):
    r = 1.0 / (d[0][0] * d[1][1] - d[0][1] * d[0][1])
    a00, a01, a11 = d[1][1] * r, -d[0][1] * r, d[0][0] * r
    x = [[a00 * d[0][2 + j] + a01 * d[1][2 + j] for j in range(2)], [a01 * d[0][2 + j] + a11 * d[1][2 + j] for j in range(2)]]
    s00 = d[2][2] - (d[0][2] * x[0][0] + d[1][2] * x[1][0])
    s01 = d[2][3] - (d[0][2] * x[0][1] + d[1][2] * x[1][1])
    s11 = d[3][3] - (d[0][3] * x[0][1] + d[1][3] * x[1][1])
    q = 1.0 / (s00 * s11 - s01 * s01)
    c00, c01, c11 = s11 * q, -s01 * q, s00 * q
    y = [[x[i][0] * c00 + x[i][1] * c01, x[i][0] * c01 + x[i][1] * c11] for i in range(2)]
    t00 = a00 + y[0][0] * x[0][0] + y[0][1] * x[0][1]
    t01 = a01 + y[0][0] * x[1][0] + y[0][1] * x[1][1]
    t11 = a11 + y[1][0] * x[1][0] + y[1][1] * x[1][1]
    return [
        [t00, t01, -y[0][0], -y[0][1]],
        [t01, t11, -y[1][0], -y[1][1]],
        [-y[0][0], -y[1][0], c00, c01],
        [-y[0][1], -y[1][1], c01, c11],
    ]


def inverse(a):
    n = a.shape[0]
    group, block = 8, 4
    lane = lax.broadcasted_iota(jnp.int32, (n, n), 1)
    sub = lax.broadcasted_iota(jnp.int32, (n, n), 0)
    lane1 = lax.broadcasted_iota(jnp.int32, (1, n), 1)

    def sweep(g, a):
        for k in range(0, group, block):
            span = range(block)
            d = [[None] * block for _ in span]
            for i in span:
                for j in range(i, block):
                    d[i][j] = jnp.broadcast_to(a[k + i : k + i + 1, k + j : k + j + 1], (1, n))
            inv = inverse_small(d)
            inside1 = (lane1 >= k) & (lane1 < k + block)
            right = [
                jnp.where(lane1 == k + j, -1.0, jnp.where(inside1, 0.0, a[k + j : k + j + 1, :])) for j in span
            ]
            insub = (sub >= k) & (sub < k + block)
            new = jnp.where(insub | ((lane >= k) & (lane < k + block)), 0.0, a)
            for i in span:
                row = inv[i][0] * right[0]
                for j in range(1, block):
                    row = row + inv[i][j] * right[j]
                col = jnp.broadcast_to(a[:, k + i : k + i + 1], (n, n))
                col = jnp.where(sub == k + i, -1.0, jnp.where(insub, 0.0, col))
                new = new - col * row
            a = new
        a = jnp.concatenate([a[group:], a[:group]], axis=0)
        return pltpu.roll(a, n - group, 1)

    return -lax.fori_loop(0, n // group, sweep, a)


def finish_kernel(
    perms, qperm, partial, basis, parent,
    mine, hold, ksend, kin, sibling, wown, win, bout, bin_,
    load_sem, k_s, k_r, s_s, s_r, w_s, w_r, b_s, b_r,
):
    c = lax.axis_index("col")
    leaf = hold.shape[1]
    peers = col_peers()
    n = len(peers)

    def load(i, j):
        return pltpu.make_async_copy(
            partial.at[pl.ds(pl.multiple_of(j * leaf, leaf), leaf)], hold.at[i], load_sem.at[i]
        )

    order = peers + [c]
    for i, j in enumerate(order):
        load(i, j).start()
    barrier = pltpu.get_barrier_semaphore()
    for j in peers:
        pl.semaphore_signal(barrier, inc=1, device_id={"col": j}, device_id_type=MESH)

    def copy(src, dst, send_sem, recv_sem, j):
        return pltpu.make_async_remote_copy(
            src_ref=src, dst_ref=dst, send_sem=send_sem, recv_sem=recv_sem,
            device_id={"col": j}, device_id_type=MESH,
        )

    rank, width = mine.shape
    lanes = lax.broadcasted_iota(jnp.int32, (rank, leaf), 1)

    def pick(i, j):
        hot = jnp.where(lanes == perms[j], 1.0, 0.0).astype(BF16)
        return jnp.dot(hot, hold[i], preferred_element_type=F32)

    kc = []
    for i, j in enumerate(peers):
        load(i, j).wait()
        ksend[i] = pick(i, j).astype(BF16)
        if i == 0:
            pl.semaphore_wait(barrier, n)
        cp = copy(ksend.at[i], kin.at[i], k_s.at[i], k_r.at[i], j)
        cp.start()
        kc.append(cp)
    load(n, c).wait()
    total = pick(n, c)
    for cp in kc:
        cp.wait_recv()
    for i in range(n):
        total = total + kin[i].astype(F32)
    mine[...] = total.astype(BF16)
    to_sibling = copy(mine, sibling, s_s, s_r, c + 1 - 2 * lax.rem(c, 2))
    to_sibling.start()

    skel = mine[...]
    wown[...] = jnp.dot(
        inverse(dot_t(skel, skel)), skel.astype(F32), precision=HI, preferred_element_type=F32
    ).astype(BF16)
    wc = []
    for i, j in enumerate(peers):
        cp = copy(wown, win.at[i], w_s.at[i], w_r.at[i], j)
        cp.start()
        wc.append(cp)

    tile = 512

    def own_rows(t, carry):
        at = pl.ds(pl.multiple_of(t * tile, tile), tile)
        basis[at, :] = dot_t(hold[n, at, :], wown[...])
        return carry

    lax.fori_loop(0, leaf // tile, own_rows, 0)

    back = [OFFSETS.index(((2 - dz) % 2, (4 - dx) % 4)) for dz, dx in OFFSETS]
    bc = []
    for i in range(n):
        wc[back[i]].wait_recv()
        cp = copy(bout.at[i], bin_.at[i], b_s.at[i], b_r.at[i], peers[i])

        def rows(t, carry, i=i):
            at = pl.ds(pl.multiple_of(t * tile, tile), tile)
            bout[i, at, :] = dot_t(hold[i, at, :], win[back[i]]).astype(BF16)
            return carry

        lax.fori_loop(0, leaf // tile, rows, 0)
        cp.start()
        bc.append(cp)

    to_sibling.wait()
    odd = lax.rem(c, 2)
    other = sibling[...]
    low = jnp.where(odd == 0, skel, other)
    high = jnp.where(odd == 0, other, skel)
    both = jnp.concatenate([low, high], axis=0)
    lanes2 = lax.broadcasted_iota(jnp.int32, (rank, 2 * rank), 1)
    hot = jnp.where(lanes2 == qperm[...], 1.0, 0.0).astype(BF16)
    chosen = jnp.dot(hot, both, preferred_element_type=F32).astype(BF16)
    parent[...] = jnp.dot(
        dot_t(skel, chosen), inverse(dot_t(chosen, chosen)), precision=HI, preferred_element_type=F32
    )

    for i in range(n):
        bc[i].wait_recv()

    def add(t, carry):
        at = pl.ds(pl.multiple_of(t * tile, tile), tile)
        value = basis[at, :]
        for i in range(n):
            value = value + bin_[i, at, :].astype(F32)
        basis[at, :] = value
        return carry

    lax.fori_loop(0, leaf // tile, add, 0)
    for cp in kc + wc + bc:
        cp.wait_send()


def finish(perms, qperm, partial):
    count, rank = perms.shape
    width = partial.shape[1]
    leaf = partial.shape[0] // count
    n = count - 1
    dma = pltpu.SemaphoreType.DMA
    return pl.pallas_call(
        finish_kernel,
        name="finish",
        out_shape=(
            jax.ShapeDtypeStruct((leaf, rank), F32),
            jax.ShapeDtypeStruct((rank, rank), F32),
        ),
        in_specs=[VMEM, VMEM, HBM],
        out_specs=(VMEM, VMEM),
        scratch_shapes=[
            pltpu.VMEM((rank, width), BF16),
            pltpu.VMEM((count, leaf, width), BF16),
            pltpu.VMEM((n, rank, width), BF16),
            pltpu.VMEM((n, rank, width), BF16),
            pltpu.VMEM((rank, width), BF16),
            pltpu.VMEM((rank, width), BF16),
            pltpu.VMEM((n, rank, width), BF16),
            pltpu.VMEM((n, leaf, rank), BF16),
            pltpu.VMEM((n, leaf, rank), BF16),
            dma((count,)), dma((n,)), dma((n,)), dma, dma,
            dma((n,)), dma((n,)), dma((n,)), dma((n,)),
        ],
        compiler_params=pltpu.CompilerParams(
            collective_id=1, has_side_effects=True, vmem_limit_bytes=40 << 20
        ),
    )(perms[:, :, None], qperm[:, None], partial)


def local(blocks, block_row, block_col, random_cols, leaf_perm, parent_perm):
    n_col = lax.axis_size("col")
    leaf_rows, width = random_cols.shape[2:]
    size = blocks.shape[1]
    nrows = leaf_rows * n_col // size
    rank = parent_perm.shape[1] // 2
    slots, steps, total = schedule(block_row, block_col, nrows)
    own_perm = jnp.broadcast_to(leaf_perm[:, :rank], (8, rank))
    gathered, perms = gather(random_cols.reshape(leaf_rows, width), own_perm)
    partial_value = spmm(slots, steps, total, blocks, gathered.reshape(-1, size, width), nrows)
    device = lax.axis_index("row") * n_col + lax.axis_index("col")
    qperm = lax.dynamic_index_in_dim(parent_perm, device // 2, 0, keepdims=False)[:rank]
    return finish(perms[:, 0], qperm, partial_value.reshape(nrows * size, width))


def solution(mesh):
    in_specs = (
        P(("row", "col"), None, None),
        P(("row", "col")),
        P(("row", "col")),
        P("col", "row", None, None),
        P(("row", "col"), None),
        P(),
    )
    out_specs = (P(("row", "col"), None), P(("row", "col"), None))
    return jax.shard_map(local, mesh=mesh, in_specs=in_specs, out_specs=out_specs, check_vma=False)
```

```python
import functools

import jax
import jax.numpy as jnp
from jax import lax
from jax.experimental import pallas as pl
from jax.experimental.pallas import tpu as pltpu
from jax.sharding import PartitionSpec as P

HI = lax.Precision.HIGHEST
VMEM = pl.BlockSpec(memory_space=pltpu.VMEM)
SMEM = pl.BlockSpec(memory_space=pltpu.SMEM)
HBM = pl.BlockSpec(memory_space=pltpu.HBM)
F32 = jnp.float32
BF16 = jnp.bfloat16


def schedule(rows, cols):
    count, lanes = rows.shape[1], 128
    nrows, steps = 128, 256

    def iota(shape, dim):
        return lax.broadcasted_iota(jnp.int32, shape, dim)

    def ones(mask):
        return jnp.where(mask, 1, 0)

    def down(value):
        return jnp.broadcast_to(value, (lanes, count)).T

    rows_k, cols_k = down(rows), down(cols)
    lane = iota((count, lanes), 1)
    sub = iota((count, lanes), 0)
    within = jnp.zeros((count, 1), jnp.int32)
    for part in range(count // lanes):
        other = jnp.broadcast_to(rows[:, part * lanes : (part + 1) * lanes], (count, lanes))
        same = (other == rows_k) & (lane + part * lanes < sub)
        within = within + jnp.sum(ones(same), axis=1, keepdims=True)
    held = jnp.sum(ones(rows_k == lane), axis=0, keepdims=True)
    pairs = lax.shift_right_logical(held + 1, 1)
    base = jnp.sum(jnp.where(lane < rows_k, jnp.broadcast_to(pairs, (count, lanes)), 0), axis=1, keepdims=True)
    place = jnp.broadcast_to(2 * base + within, (count, lanes))
    code = (sub + 1) * 65536 + cols_k
    lane_r, sub_r = iota((nrows, lanes), 1), iota((nrows, lanes), 0)
    pairs_all = jnp.broadcast_to(pairs, (nrows, lanes))
    before = jnp.broadcast_to(
        jnp.sum(jnp.where(lane_r < sub_r, pairs_all, 0), axis=1, keepdims=True), (nrows, lanes)
    )
    end = before + jnp.broadcast_to(
        jnp.sum(jnp.where(lane_r == sub_r, pairs_all, 0), axis=1, keepdims=True), (nrows, lanes)
    )
    out = []
    for part in range(2 * steps // lanes):
        out.append(jnp.sum(jnp.where(place == lane + part * lanes, code, 0), axis=0, keepdims=True))
    for part in range(steps // lanes):
        q = lane_r + part * lanes
        row = jnp.minimum(jnp.sum(ones(end <= q), axis=0, keepdims=True), nrows - 1)
        out.append(2 * row + jnp.sum(ones(before == q), axis=0, keepdims=True))
    total = jnp.sum(jnp.where(sub_r == 0, jnp.broadcast_to(jnp.max(end, axis=0, keepdims=True), (nrows, lanes)), 0), axis=0, keepdims=True)
    return out + [total, jnp.zeros_like(total)]


MESH = pl.DeviceIdType.MESH


OFFSETS = ((1, 2), (0, 2), (1, 1), (1, 3), (0, 1), (0, 3), (1, 0))


def col_peers():
    c = lax.axis_index("col")
    zh, x = c // 4, lax.rem(c, 4)
    return [lax.rem(zh + dz, 2) * 4 + lax.rem(x + dx, 4) for dz, dx in OFFSETS]


def gather_kernel(
    own, ints, out, perms, plan,
    perm, local_sem, send_sem, recv_sem, core_send, core_recv, perm_local, perm_send, perm_recv,
):
    r = lax.axis_index("row")
    y, zl, co = r // 4, lax.rem(r // 2, 2), lax.rem(r, 2)
    size = own.shape[0]
    half = size // 2
    low = size * 7 // 16
    mid = low + (size - low) // 2

    def at(dy, dz, dc=0):
        return lax.rem(y + dy + 4, 4) * 4 + lax.rem(zl + dz, 2) * 2 + lax.rem(co + dc, 2)

    up, down, side, core = at(1, 0), at(-1, 0), at(0, 1), at(0, 0, 1)
    barrier = pltpu.get_barrier_semaphore()
    for peer in (up, down, side, core):
        pl.semaphore_signal(barrier, inc=1, device_id={"row": peer}, device_id_type=MESH)
    peers = col_peers()
    for j in peers:
        pl.semaphore_signal(barrier, inc=1, device_id={"col": j}, device_id_type=MESH)
    keep = pltpu.make_async_copy(own, out.at[pl.ds(pl.multiple_of(r * size, size), size)], local_sem)
    keep.start()
    n_blocks = (ints.shape[1] - perm.shape[1]) // 2
    perm[...] = jnp.broadcast_to(ints[:, 2 * n_blocks :], perm.shape)
    keep_perm = pltpu.make_async_copy(perm, perms.at[lax.axis_index("col")], perm_local)
    keep_perm.start()
    pl.semaphore_wait(barrier, 4 + len(peers))

    def rows(source, first, last):
        return pl.ds(pl.multiple_of(source * size + first, 16), last - first)

    sent = []

    def send(source, first, last, target, slot, mine=False):
        dst = out.at[rows(source, first, last)]
        cp = pltpu.make_async_remote_copy(
            src_ref=own.at[pl.ds(first, last - first)] if mine else dst,
            dst_ref=dst,
            send_sem=send_sem.at[len(sent)],
            recv_sem=recv_sem.at[slot],
            device_id={"row": target},
            device_id_type=MESH,
        )
        cp.start()
        sent.append(cp)
        return cp

    crossed = []

    def cross(source, first, last, mine=False):
        dst = out.at[rows(source, first, last)]
        cp = pltpu.make_async_remote_copy(
            src_ref=own if mine else dst,
            dst_ref=dst,
            send_sem=core_send.at[len(crossed)],
            recv_sem=core_recv.at[len(crossed)],
            device_id={"row": core},
            device_id_type=MESH,
        )
        cp.start()
        crossed.append(cp)

    def arrived(source, first, last, slot):
        dst = out.at[rows(source, first, last)]
        pltpu.make_async_remote_copy(
            src_ref=dst,
            dst_ref=dst,
            send_sem=send_sem.at[0],
            recv_sem=recv_sem.at[slot],
            device_id={"row": core},
            device_id_type=MESH,
        ).wait_recv()

    send(r, 0, half, up, 0, True)
    send(r, half, size, down, 2, True)
    send(r, low, size, side, 4, True)
    send(r, half, size, up, 1, True)
    send(r, 0, half, down, 3, True)
    send(r, 0, low, side, 5, True)
    cross(r, 0, size, True)
    orders = []
    for i, j in enumerate(peers):
        cp = pltpu.make_async_remote_copy(
            src_ref=perm,
            dst_ref=perms.at[lax.axis_index("col")],
            send_sem=perm_send.at[i],
            recv_sem=perm_recv.at[i],
            device_id={"col": j},
            device_id_type=MESH,
        )
        cp.start()
        orders.append(cp)
    for i, value in enumerate(schedule(ints[:, :n_blocks], ints[:, n_blocks : 2 * n_blocks])):
        plan[i : i + 1, :] = value

    prev, nxt, far = at(-1, 0), at(1, 0), at(2, 0)
    zown, zprev, znext, zfar = at(0, 1), at(-1, 1), at(1, 1), at(2, 1)

    arrived(prev, 0, half, 0)
    far_up = send(prev, 0, half, up, 6)
    send(prev, 0, low, side, 10)
    cross(prev, 0, half)
    arrived(nxt, half, size, 2)
    far_down = send(nxt, half, size, down, 7)
    cross(nxt, half, size)
    arrived(nxt, 0, half, 3)
    send(nxt, 0, low, side, 11)
    cross(nxt, 0, half)
    arrived(prev, half, size, 1)
    cross(prev, half, size)
    arrived(zown, low, size, 4)
    cross(zown, low, size)
    arrived(zown, 0, low, 5)
    cross(zown, 0, low)
    far_up.wait_send()
    send(zown, low, size, up, 8)
    far_down.wait_send()
    send(zown, low, size, down, 9)
    arrived(far, 0, half, 6)
    send(far, 0, low, side, 14)
    cross(far, 0, half)
    arrived(far, half, size, 7)
    cross(far, half, size)
    arrived(zprev, low, size, 8)
    send(zprev, low, mid, up, 12)
    cross(zprev, low, size)
    arrived(znext, low, size, 9)
    send(znext, mid, size, down, 13)
    cross(znext, low, size)
    arrived(zprev, 0, low, 10)
    cross(zprev, 0, low)
    arrived(znext, 0, low, 11)
    cross(znext, 0, low)
    arrived(zfar, low, mid, 12)
    cross(zfar, low, mid)
    arrived(zfar, mid, size, 13)
    cross(zfar, mid, size)
    arrived(zfar, 0, low, 14)
    cross(zfar, 0, low)
    keep.wait()
    keep_perm.wait()
    for cp in orders:
        cp.wait()
    for cp in sent:
        if cp is not far_up and cp is not far_down:
            cp.wait_send()
    for cp in crossed:
        cp.wait()


def gather(own, rows, cols, order):
    size, width = own.shape
    count, n_col = lax.axis_size("row"), lax.axis_size("col")
    rank = order.shape[0]
    ints = jnp.concatenate([rows, cols, order])[None, :]
    dma = pltpu.SemaphoreType.DMA
    return pl.pallas_call(
        gather_kernel,
        name="gather",
        out_shape=(
            jax.ShapeDtypeStruct((count * size, width), own.dtype),
            jax.ShapeDtypeStruct((n_col, 8, rank), jnp.int32),
            jax.ShapeDtypeStruct((8, 128), jnp.int32),
        ),
        in_specs=[HBM, VMEM],
        out_specs=(HBM, HBM, VMEM),
        scratch_shapes=[
            pltpu.VMEM((8, rank), jnp.int32),
            dma, dma((16,)), dma((15,)), dma((16,)), dma((16,)), dma, dma((n_col - 1,)), dma((n_col - 1,)),
        ],
        compiler_params=pltpu.CompilerParams(
            collective_id=0, has_side_effects=True, vmem_limit_bytes=4 << 20
        ),
        cost_estimate=pl.CostEstimate(flops=60000000000, bytes_accessed=40000000, transcendentals=0),
    )(own, ints)


UNROLL = 4


def spmm_kernel(plan, blocks, rand, out, acc):
    acc[...] = jnp.zeros_like(acc)
    size = acc.shape[0]
    per = out.shape[1] // size

    def pair(q):
        mats, rights = [], []
        for s in range(2):
            t = 2 * q + s
            code = plan[t // 128, lax.rem(t, 128)]
            k = jnp.maximum(lax.shift_right_logical(code, 16) - 1, 0)
            col = jnp.bitwise_and(code, 65535)
            mat = blocks[k]
            mats.append(jnp.where(code > 0, mat, jnp.zeros_like(mat)))
            rights.append(rand[col])
        return jnp.dot(
            jnp.concatenate(mats, axis=1),
            jnp.concatenate(rights, axis=0),
            preferred_element_type=F32,
        )

    def body(g, carry):
        prods = [pair(g * UNROLL + u) for u in range(UNROLL)]
        for u in range(UNROLL):
            q = g * UNROLL + u
            info = plan[4 + q // 128, lax.rem(q, 128)]
            keep = (1 - jnp.bitwise_and(info, 1)).astype(F32)
            value = acc[...] * keep + prods[u]
            acc[...] = value
            row = lax.shift_right_logical(info, 1)
            at = pl.multiple_of(lax.rem(row, per) * size, size)
            out[row // per, pl.ds(at, size), :] = value.astype(BF16)
        return carry

    lax.fori_loop(0, (plan[6, 0] + UNROLL - 1) // UNROLL, body, 0)


def spmm(plan, blocks, rand, leaves, leaf_rows):
    size, width = blocks.shape[1], rand.shape[2]
    return pl.pallas_call(
        spmm_kernel,
        name="spmm",
        out_shape=jax.ShapeDtypeStruct((leaves, leaf_rows, width), BF16),
        in_specs=[SMEM, VMEM, VMEM],
        out_specs=VMEM,
        scratch_shapes=[pltpu.VMEM((size, width), F32)],
        compiler_params=pltpu.CompilerParams(vmem_limit_bytes=4 << 20),
    )(plan, blocks, rand)


def dot_t(a, b):
    return lax.dot_general(a, b, (((1,), (1,)), ((), ())), preferred_element_type=F32)


def inverse_small(d):
    r = 1.0 / (d[0][0] * d[1][1] - d[0][1] * d[0][1])
    a00, a01, a11 = d[1][1] * r, -d[0][1] * r, d[0][0] * r
    x = [[a00 * d[0][2 + j] + a01 * d[1][2 + j] for j in range(2)], [a01 * d[0][2 + j] + a11 * d[1][2 + j] for j in range(2)]]
    s00 = d[2][2] - (d[0][2] * x[0][0] + d[1][2] * x[1][0])
    s01 = d[2][3] - (d[0][2] * x[0][1] + d[1][2] * x[1][1])
    s11 = d[3][3] - (d[0][3] * x[0][1] + d[1][3] * x[1][1])
    q = 1.0 / (s00 * s11 - s01 * s01)
    c00, c01, c11 = s11 * q, -s01 * q, s00 * q
    y = [[x[i][0] * c00 + x[i][1] * c01, x[i][0] * c01 + x[i][1] * c11] for i in range(2)]
    t00 = a00 + y[0][0] * x[0][0] + y[0][1] * x[0][1]
    t01 = a01 + y[0][0] * x[1][0] + y[0][1] * x[1][1]
    t11 = a11 + y[1][0] * x[1][0] + y[1][1] * x[1][1]
    return [
        [t00, t01, -y[0][0], -y[0][1]],
        [t01, t11, -y[1][0], -y[1][1]],
        [-y[0][0], -y[1][0], c00, c01],
        [-y[0][1], -y[1][1], c01, c11],
    ]


def inverse(a):
    n = a.shape[0]
    group, block = 8, 4
    lane = lax.broadcasted_iota(jnp.int32, (n, n), 1)
    sub = lax.broadcasted_iota(jnp.int32, (n, n), 0)
    lane1 = lax.broadcasted_iota(jnp.int32, (1, n), 1)

    def sweep(g, a):
        for k in range(0, group, block):
            span = range(block)
            d = [[None] * block for _ in span]
            for i in span:
                for j in range(i, block):
                    d[i][j] = jnp.broadcast_to(a[k + i : k + i + 1, k + j : k + j + 1], (1, n))
            inv = inverse_small(d)
            inside1 = (lane1 >= k) & (lane1 < k + block)
            right = [
                jnp.where(lane1 == k + j, -1.0, jnp.where(inside1, 0.0, a[k + j : k + j + 1, :])) for j in span
            ]
            insub = (sub >= k) & (sub < k + block)
            new = jnp.where(insub | ((lane >= k) & (lane < k + block)), 0.0, a)
            for i in span:
                row = inv[i][0] * right[0]
                for j in range(1, block):
                    row = row + inv[i][j] * right[j]
                col = jnp.broadcast_to(a[:, k + i : k + i + 1], (n, n))
                col = jnp.where(sub == k + i, -1.0, jnp.where(insub, 0.0, col))
                new = new - col * row
            a = new
        a = jnp.concatenate([a[group:], a[:group]], axis=0)
        return pltpu.roll(a, n - group, 1)

    return -lax.fori_loop(0, n // group, sweep, a)


def finish_kernel(
    perms, parent_perm, partial, basis, parent,
    mine, ksend, kin, sibling, wown, win, zout, zin, xout, xin, yout, yin, vout, vin,
    k_s, k_r, s_s, s_r, w_s, w_r, z_s, z_r, x_s, x_r, y_s, y_r, v_s, v_r,
):
    c = lax.axis_index("col")
    zh, x = c // 4, lax.rem(c, 4)
    leaf = partial.shape[1]
    peers = col_peers()
    n = len(peers)
    rank, width = mine.shape
    cut = zout.shape[1]
    tile = 256

    barrier = pltpu.get_barrier_semaphore()
    for j in peers:
        pl.semaphore_signal(barrier, inc=1, device_id={"col": j}, device_id_type=MESH)

    def copy(src, dst, send_sem, recv_sem, j):
        return pltpu.make_async_remote_copy(
            src_ref=src, dst_ref=dst, send_sem=send_sem, recv_sem=recv_sem,
            device_id={"col": j}, device_id_type=MESH,
        )

    lanes = lax.broadcasted_iota(jnp.int32, (rank, leaf), 1)

    def down(row):
        return jnp.broadcast_to(row, (rank, rank)).T[:, :1]

    def pick(j):
        hot = jnp.where(lanes == down(perms[j, 0:1, :]), 1.0, 0.0).astype(BF16)
        return jnp.dot(hot, partial[j], preferred_element_type=F32)

    kc = []
    for i, j in enumerate(peers):
        ksend[i] = pick(j).astype(BF16)
        if i == 0:
            pl.semaphore_wait(barrier, n)
        cp = copy(ksend.at[i], kin.at[i], k_s.at[i], k_r.at[i], j)
        cp.start()
        kc.append(cp)
    total = pick(c)
    for cp in kc:
        cp.wait_recv()
    for i in range(n):
        total = total + kin[i].astype(F32)
    mine[...] = total.astype(BF16)
    to_sibling = copy(mine, sibling, s_s, s_r, c + 1 - 2 * lax.rem(c, 2))
    to_sibling.start()

    skel = mine[...]
    wown[...] = jnp.dot(
        inverse(dot_t(skel, skel)), skel.astype(F32), precision=HI, preferred_element_type=F32
    ).astype(BF16)
    wc = []
    for i, j in enumerate(peers):
        cp = copy(wown, win.at[i], w_s.at[i], w_r.at[i], j)
        cp.start()
        wc.append(cp)

    def times(j, first, last, weight, put):
        def rows(t, carry):
            at = pl.multiple_of(t * tile, tile)
            put(pl.ds(at, tile), dot_t(partial[j, pl.ds(first + at, tile), :], weight[...]))
            return carry

        lax.fori_loop(0, (last - first) // tile, rows, 0)

    def store(ref):
        def put(at, value):
            ref[at, :] = value.astype(ref.dtype)

        return put

    times(c, 0, leaf, wown, store(basis))

    piece = {o: OFFSETS.index(((2 - o[0]) % 2, (4 - o[1]) % 4)) for o in OFFSETS}
    at_x = [lax.rem(x + d, 4) for d in range(4)]
    zpeer = (1 - zh) * 4 + x
    zc, xc = {}, {}
    for d in (2, 1, 3, 0):
        wc[piece[(1, d)]].wait_recv()
        weight = win.at[piece[(1, d)]]
        j = (1 - zh) * 4 + at_x[d]
        times(j, 0, cut, weight, store(zout.at[d]))
        zc[d] = copy(zout.at[d], zin.at[d], z_s.at[d], z_r.at[d], zpeer)
        zc[d].start()
        if d == 0:
            continue
        times(j, cut, leaf, weight, store(xout.at[d - 1, 1]))
        xc[d, 1] = copy(xout.at[d - 1, 1], xin.at[d - 1, 1], x_s.at[d - 1, 1], x_r.at[d - 1, 1], zh * 4 + at_x[d])
        xc[d, 1].start()
        wc[piece[(0, d)]].wait_recv()
        times(zh * 4 + at_x[d], cut, leaf, win.at[piece[(0, d)]], store(xout.at[d - 1, 0]))
        xc[d, 0] = copy(xout.at[d - 1, 0], xin.at[d - 1, 0], x_s.at[d - 1, 0], x_r.at[d - 1, 0], zh * 4 + at_x[d])
        xc[d, 0].start()

    to_sibling.wait()
    odd = lax.rem(c, 2)
    other = sibling[...]
    both = jnp.concatenate([jnp.where(odd == 0, skel, other), jnp.where(odd == 0, other, skel)], axis=0)
    lanes2 = lax.broadcasted_iota(jnp.int32, (rank, 2 * rank), 1)
    order = parent_perm[pl.ds((lax.axis_index("row") * (n + 1) + c) // 2, 1), :]
    hot = jnp.where(lanes2 == down(order[:, :rank]), 1.0, 0.0).astype(BF16)
    chosen = jnp.dot(hot, both, preferred_element_type=F32).astype(BF16)
    parent[...] = jnp.dot(
        dot_t(skel, chosen), inverse(dot_t(chosen, chosen)), precision=HI, preferred_element_type=F32
    )

    yc = {}
    for d in (2, 1, 3):
        zc[d].wait_recv()

        def put(at, value, d=d):
            yout[d - 1, at, :] = (value + zin[d, at, :].astype(F32)).astype(BF16)

        times(zh * 4 + at_x[d], 0, cut, win.at[piece[(0, d)]], put)
        yc[d] = copy(yout.at[d - 1], yin.at[d - 1], y_s.at[d - 1], y_r.at[d - 1], zh * 4 + at_x[d])
        yc[d].start()
        if d == 1:
            for e in (2, 1, 3):
                xc[e, 1].wait_recv()

            def put_v(at, value):
                for e in range(3):
                    value = value + xin[e, 1, at, :].astype(F32)
                vout[at, :] = value.astype(BF16)

            times(zpeer, cut, leaf, win.at[piece[(1, 0)]], put_v)
            vc = copy(vout, vin, v_s, v_r, zpeer)
            vc.start()

    for e in (2, 1, 3):
        xc[e, 0].wait_recv()
    zc[0].wait_recv()
    vc.wait_recv()

    def add_high(t, carry):
        at = pl.multiple_of(t * tile, tile)
        value = basis[pl.ds(cut + at, tile), :] + vin[pl.ds(at, tile), :].astype(F32)
        for e in range(3):
            value = value + xin[e, 0, pl.ds(at, tile), :].astype(F32)
        basis[pl.ds(cut + at, tile), :] = value
        return carry

    lax.fori_loop(0, (leaf - cut) // tile, add_high, 0)
    for d in (2, 1, 3):
        yc[d].wait_recv()

    def add_low(t, carry):
        at = pl.ds(pl.multiple_of(t * tile, tile), tile)
        value = basis[at, :] + zin[0, at, :].astype(F32)
        for e in range(3):
            value = value + yin[e, at, :].astype(F32)
        basis[at, :] = value
        return carry

    lax.fori_loop(0, cut // tile, add_low, 0)
    for cp in kc + wc + list(zc.values()) + list(xc.values()) + list(yc.values()) + [vc]:
        cp.wait_send()


def finish(perms, parent_perm, partial):
    count, _, rank = perms.shape
    leaf, width = partial.shape[1:]
    n = count - 1
    cut = leaf * 5 // 8
    dma = pltpu.SemaphoreType.DMA
    return pl.pallas_call(
        finish_kernel,
        name="finish",
        out_shape=(
            jax.ShapeDtypeStruct((leaf, rank), F32),
            jax.ShapeDtypeStruct((rank, rank), F32),
        ),
        in_specs=[VMEM, VMEM, VMEM],
        out_specs=(VMEM, VMEM),
        scratch_shapes=[
            pltpu.VMEM((rank, width), BF16),
            pltpu.VMEM((n, rank, width), BF16),
            pltpu.VMEM((n, rank, width), BF16),
            pltpu.VMEM((rank, width), BF16),
            pltpu.VMEM((rank, width), BF16),
            pltpu.VMEM((n, rank, width), BF16),
            pltpu.VMEM((4, cut, rank), BF16),
            pltpu.VMEM((4, cut, rank), BF16),
            pltpu.VMEM((3, 2, leaf - cut, rank), BF16),
            pltpu.VMEM((3, 2, leaf - cut, rank), BF16),
            pltpu.VMEM((3, cut, rank), BF16),
            pltpu.VMEM((3, cut, rank), BF16),
            pltpu.VMEM((leaf - cut, rank), BF16),
            pltpu.VMEM((leaf - cut, rank), BF16),
            dma((n,)), dma((n,)), dma, dma, dma((n,)), dma((n,)),
            dma((4,)), dma((4,)), dma((3, 2)), dma((3, 2)), dma((3,)), dma((3,)), dma, dma,
        ],
        compiler_params=pltpu.CompilerParams(
            collective_id=1, has_side_effects=True, vmem_limit_bytes=24 << 20
        ),
    )(perms, parent_perm, partial)


def local(blocks, block_row, block_col, random_cols, leaf_perm, parent_perm):
    n_col = lax.axis_size("col")
    leaf_rows, width = random_cols.shape[2:]
    size = blocks.shape[1]
    rank = parent_perm.shape[1] // 2
    gathered, perms, plan = gather(
        random_cols.reshape(leaf_rows, width), block_row, block_col, leaf_perm[0, :rank]
    )
    partial_value = spmm(plan, blocks, gathered.reshape(-1, size, width), n_col, leaf_rows)
    return finish(perms, parent_perm, partial_value)


def solution(mesh):
    in_specs = (
        P(("row", "col"), None, None),
        P(("row", "col")),
        P(("row", "col")),
        P("col", "row", None, None),
        P(("row", "col"), None),
        P(),
    )
    out_specs = (P(("row", "col"), None), P(("row", "col"), None))
    return jax.shard_map(local, mesh=mesh, in_specs=in_specs, out_specs=out_specs, check_vma=False)
```

```python
import functools

import jax
import jax.numpy as jnp
from jax import lax
from jax.experimental import pallas as pl
from jax.experimental.pallas import tpu as pltpu
from jax.sharding import PartitionSpec as P

HI = lax.Precision.HIGHEST
VMEM = pl.BlockSpec(memory_space=pltpu.VMEM)
SMEM = pl.BlockSpec(memory_space=pltpu.SMEM)
HBM = pl.BlockSpec(memory_space=pltpu.HBM)
F32 = jnp.float32
BF16 = jnp.bfloat16


def schedule(rows, cols):
    count, lanes = rows.shape[1], 128
    nrows, steps = 128, 256

    def iota(shape, dim):
        return lax.broadcasted_iota(jnp.int32, shape, dim)

    def ones(mask):
        return jnp.where(mask, 1, 0)

    def down(value):
        return jnp.broadcast_to(value, (lanes, count)).T

    rows_k, cols_k = down(rows), down(cols)
    lane = iota((count, lanes), 1)
    sub = iota((count, lanes), 0)
    within = jnp.zeros((count, 1), jnp.int32)
    for part in range(count // lanes):
        other = jnp.broadcast_to(rows[:, part * lanes : (part + 1) * lanes], (count, lanes))
        same = (other == rows_k) & (lane + part * lanes < sub)
        within = within + jnp.sum(ones(same), axis=1, keepdims=True)
    held = jnp.sum(ones(rows_k == lane), axis=0, keepdims=True)
    pairs = lax.shift_right_logical(held + 1, 1)
    base = jnp.sum(jnp.where(lane < rows_k, jnp.broadcast_to(pairs, (count, lanes)), 0), axis=1, keepdims=True)
    place = jnp.broadcast_to(2 * base + within, (count, lanes))
    code = (sub + 1) * 65536 + cols_k
    lane_r, sub_r = iota((nrows, lanes), 1), iota((nrows, lanes), 0)
    pairs_all = jnp.broadcast_to(pairs, (nrows, lanes))
    before = jnp.broadcast_to(
        jnp.sum(jnp.where(lane_r < sub_r, pairs_all, 0), axis=1, keepdims=True), (nrows, lanes)
    )
    end = before + jnp.broadcast_to(
        jnp.sum(jnp.where(lane_r == sub_r, pairs_all, 0), axis=1, keepdims=True), (nrows, lanes)
    )
    out = []
    for part in range(2 * steps // lanes):
        out.append(jnp.sum(jnp.where(place == lane + part * lanes, code, 0), axis=0, keepdims=True))
    for part in range(steps // lanes):
        q = lane_r + part * lanes
        row = jnp.minimum(jnp.sum(ones(end <= q), axis=0, keepdims=True), nrows - 1)
        out.append(2 * row + jnp.sum(ones(before == q), axis=0, keepdims=True))
    total = jnp.sum(jnp.where(sub_r == 0, jnp.broadcast_to(jnp.max(end, axis=0, keepdims=True), (nrows, lanes)), 0), axis=0, keepdims=True)
    return out + [total, jnp.zeros_like(total)]


MESH = pl.DeviceIdType.MESH


OFFSETS = ((1, 2), (0, 2), (1, 1), (1, 3), (0, 1), (0, 3), (1, 0))


def col_peers():
    c = lax.axis_index("col")
    zh, x = c // 4, lax.rem(c, 4)
    return [lax.rem(zh + dz, 2) * 4 + lax.rem(x + dx, 4) for dz, dx in OFFSETS]


def gather_kernel(
    own, ints, out, perms, plan,
    perm, local_sem, send_sem, recv_sem, core_send, core_recv, perm_local, perm_send, perm_recv,
):
    r = lax.axis_index("row")
    y, zl, co = r // 4, lax.rem(r // 2, 2), lax.rem(r, 2)
    size = own.shape[0]
    half = size // 2
    low = size * 7 // 16
    mid = low + (size - low) // 2

    def at(dy, dz, dc=0):
        return lax.rem(y + dy + 4, 4) * 4 + lax.rem(zl + dz, 2) * 2 + lax.rem(co + dc, 2)

    up, down, side, core = at(1, 0), at(-1, 0), at(0, 1), at(0, 0, 1)
    barrier = pltpu.get_barrier_semaphore()
    for peer in (up, down, side, core):
        pl.semaphore_signal(barrier, inc=1, device_id={"row": peer}, device_id_type=MESH)
    peers = col_peers()
    for j in peers:
        pl.semaphore_signal(barrier, inc=1, device_id={"col": j}, device_id_type=MESH)
    keep = pltpu.make_async_copy(own, out.at[pl.ds(pl.multiple_of(r * size, size), size)], local_sem)
    keep.start()
    n_blocks = (ints.shape[1] - perm.shape[1]) // 2
    perm[...] = jnp.broadcast_to(ints[:, 2 * n_blocks :], perm.shape)
    keep_perm = pltpu.make_async_copy(perm, perms.at[lax.axis_index("col")], perm_local)
    keep_perm.start()
    pl.semaphore_wait(barrier, 4 + len(peers))

    def rows(source, first, last):
        return pl.ds(pl.multiple_of(source * size + first, 16), last - first)

    sent = []

    def send(source, first, last, target, slot, mine=False):
        dst = out.at[rows(source, first, last)]
        cp = pltpu.make_async_remote_copy(
            src_ref=own.at[pl.ds(first, last - first)] if mine else dst,
            dst_ref=dst,
            send_sem=send_sem.at[len(sent)],
            recv_sem=recv_sem.at[slot],
            device_id={"row": target},
            device_id_type=MESH,
        )
        cp.start()
        sent.append(cp)
        return cp

    crossed = []

    def cross(source, first, last, mine=False):
        dst = out.at[rows(source, first, last)]
        cp = pltpu.make_async_remote_copy(
            src_ref=own if mine else dst,
            dst_ref=dst,
            send_sem=core_send.at[len(crossed)],
            recv_sem=core_recv.at[len(crossed)],
            device_id={"row": core},
            device_id_type=MESH,
        )
        cp.start()
        crossed.append(cp)

    def arrived(source, first, last, slot):
        dst = out.at[rows(source, first, last)]
        pltpu.make_async_remote_copy(
            src_ref=dst,
            dst_ref=dst,
            send_sem=send_sem.at[0],
            recv_sem=recv_sem.at[slot],
            device_id={"row": core},
            device_id_type=MESH,
        ).wait_recv()

    send(r, 0, half, up, 0, True)
    send(r, half, size, down, 2, True)
    send(r, low, size, side, 4, True)
    send(r, half, size, up, 1, True)
    send(r, 0, half, down, 3, True)
    send(r, 0, low, side, 5, True)
    cross(r, 0, size, True)
    orders = []
    for i, j in enumerate(peers):
        cp = pltpu.make_async_remote_copy(
            src_ref=perm,
            dst_ref=perms.at[lax.axis_index("col")],
            send_sem=perm_send.at[i],
            recv_sem=perm_recv.at[i],
            device_id={"col": j},
            device_id_type=MESH,
        )
        cp.start()
        orders.append(cp)
    for i, value in enumerate(schedule(ints[:, :n_blocks], ints[:, n_blocks : 2 * n_blocks])):
        plan[i : i + 1, :] = value

    prev, nxt, far = at(-1, 0), at(1, 0), at(2, 0)
    zown, zprev, znext, zfar = at(0, 1), at(-1, 1), at(1, 1), at(2, 1)

    arrived(prev, 0, half, 0)
    far_up = send(prev, 0, half, up, 6)
    send(prev, 0, low, side, 10)
    cross(prev, 0, half)
    arrived(nxt, half, size, 2)
    far_down = send(nxt, half, size, down, 7)
    cross(nxt, half, size)
    arrived(nxt, 0, half, 3)
    send(nxt, 0, low, side, 11)
    cross(nxt, 0, half)
    arrived(prev, half, size, 1)
    cross(prev, half, size)
    arrived(zown, low, size, 4)
    cross(zown, low, size)
    arrived(zown, 0, low, 5)
    cross(zown, 0, low)
    far_up.wait_send()
    send(zown, low, size, up, 8)
    far_down.wait_send()
    send(zown, low, size, down, 9)
    arrived(far, 0, half, 6)
    send(far, 0, low, side, 14)
    cross(far, 0, half)
    arrived(far, half, size, 7)
    cross(far, half, size)
    arrived(zprev, low, size, 8)
    send(zprev, low, mid, up, 12)
    cross(zprev, low, size)
    arrived(znext, low, size, 9)
    send(znext, mid, size, down, 13)
    cross(znext, low, size)
    arrived(zprev, 0, low, 10)
    cross(zprev, 0, low)
    arrived(znext, 0, low, 11)
    cross(znext, 0, low)
    arrived(zfar, low, mid, 12)
    cross(zfar, low, mid)
    arrived(zfar, mid, size, 13)
    cross(zfar, mid, size)
    arrived(zfar, 0, low, 14)
    cross(zfar, 0, low)
    keep.wait()
    keep_perm.wait()
    for cp in orders:
        cp.wait()
    for cp in sent:
        if cp is not far_up and cp is not far_down:
            cp.wait_send()
    for cp in crossed:
        cp.wait()


def gather(own, rows, cols, order):
    size, width = own.shape
    count, n_col = lax.axis_size("row"), lax.axis_size("col")
    rank = order.shape[0]
    ints = jnp.concatenate([rows, cols, order])[None, :]
    dma = pltpu.SemaphoreType.DMA
    return pl.pallas_call(
        gather_kernel,
        name="gather",
        out_shape=(
            jax.ShapeDtypeStruct((count * size, width), own.dtype),
            jax.ShapeDtypeStruct((n_col, 8, rank), jnp.int32),
            jax.ShapeDtypeStruct((8, 128), jnp.int32),
        ),
        in_specs=[HBM, VMEM],
        out_specs=(HBM, HBM, VMEM),
        scratch_shapes=[
            pltpu.VMEM((8, rank), jnp.int32),
            dma, dma((16,)), dma((15,)), dma((16,)), dma((16,)), dma, dma((n_col - 1,)), dma((n_col - 1,)),
        ],
        compiler_params=pltpu.CompilerParams(
            collective_id=0, has_side_effects=True, vmem_limit_bytes=4 << 20
        ),
        cost_estimate=pl.CostEstimate(flops=60000000000, bytes_accessed=40000000, transcendentals=0),
    )(own, ints)


UNROLL = 8


def spmm_kernel(plan, blocks, rand, out, acc):
    acc[...] = jnp.zeros_like(acc)
    size = acc.shape[0]
    per = out.shape[1] // size

    def pair(q):
        mats, rights = [], []
        for s in range(2):
            t = 2 * q + s
            code = plan[t // 128, lax.rem(t, 128)]
            k = jnp.maximum(lax.shift_right_logical(code, 16) - 1, 0)
            col = jnp.bitwise_and(code, 65535)
            mat = blocks[k]
            mats.append(jnp.where(code > 0, mat, jnp.zeros_like(mat)))
            rights.append(rand[col])
        return jnp.dot(
            jnp.concatenate(mats, axis=1),
            jnp.concatenate(rights, axis=0),
            preferred_element_type=F32,
        )

    def body(g, carry):
        prods = [pair(g * UNROLL + u) for u in range(UNROLL)]
        for u in range(UNROLL):
            q = g * UNROLL + u
            info = plan[4 + q // 128, lax.rem(q, 128)]
            keep = (1 - jnp.bitwise_and(info, 1)).astype(F32)
            value = acc[...] * keep + prods[u]
            acc[...] = value
            row = lax.shift_right_logical(info, 1)
            at = pl.multiple_of(lax.rem(row, per) * size, size)
            out[row // per, pl.ds(at, size), :] = value.astype(BF16)
        return carry

    lax.fori_loop(0, (plan[6, 0] + UNROLL - 1) // UNROLL, body, 0)


def spmm(plan, blocks, rand, leaves, leaf_rows):
    size, width = blocks.shape[1], rand.shape[2]
    return pl.pallas_call(
        spmm_kernel,
        name="spmm",
        out_shape=jax.ShapeDtypeStruct((leaves, leaf_rows, width), BF16),
        in_specs=[SMEM, VMEM, VMEM],
        out_specs=VMEM,
        scratch_shapes=[pltpu.VMEM((size, width), F32)],
        compiler_params=pltpu.CompilerParams(vmem_limit_bytes=4 << 20),
    )(plan, blocks, rand)


def dot_t(a, b):
    return lax.dot_general(a, b, (((1,), (1,)), ((), ())), preferred_element_type=F32)


def inverse_small(d):
    r = 1.0 / (d[0][0] * d[1][1] - d[0][1] * d[0][1])
    a00, a01, a11 = d[1][1] * r, -d[0][1] * r, d[0][0] * r
    x = [[a00 * d[0][2 + j] + a01 * d[1][2 + j] for j in range(2)], [a01 * d[0][2 + j] + a11 * d[1][2 + j] for j in range(2)]]
    s00 = d[2][2] - (d[0][2] * x[0][0] + d[1][2] * x[1][0])
    s01 = d[2][3] - (d[0][2] * x[0][1] + d[1][2] * x[1][1])
    s11 = d[3][3] - (d[0][3] * x[0][1] + d[1][3] * x[1][1])
    q = 1.0 / (s00 * s11 - s01 * s01)
    c00, c01, c11 = s11 * q, -s01 * q, s00 * q
    y = [[x[i][0] * c00 + x[i][1] * c01, x[i][0] * c01 + x[i][1] * c11] for i in range(2)]
    t00 = a00 + y[0][0] * x[0][0] + y[0][1] * x[0][1]
    t01 = a01 + y[0][0] * x[1][0] + y[0][1] * x[1][1]
    t11 = a11 + y[1][0] * x[1][0] + y[1][1] * x[1][1]
    return [
        [t00, t01, -y[0][0], -y[0][1]],
        [t01, t11, -y[1][0], -y[1][1]],
        [-y[0][0], -y[1][0], c00, c01],
        [-y[0][1], -y[1][1], c01, c11],
    ]


def inverse(a):
    n = a.shape[0]
    group, block = 8, 4
    lane = lax.broadcasted_iota(jnp.int32, (n, n), 1)
    sub = lax.broadcasted_iota(jnp.int32, (n, n), 0)
    lane1 = lax.broadcasted_iota(jnp.int32, (1, n), 1)

    def sweep(g, a):
        for k in range(0, group, block):
            span = range(block)
            d = [[None] * block for _ in span]
            for i in span:
                for j in range(i, block):
                    d[i][j] = jnp.broadcast_to(a[k + i : k + i + 1, k + j : k + j + 1], (1, n))
            inv = inverse_small(d)
            inside1 = (lane1 >= k) & (lane1 < k + block)
            right = [
                jnp.where(lane1 == k + j, -1.0, jnp.where(inside1, 0.0, a[k + j : k + j + 1, :])) for j in span
            ]
            insub = (sub >= k) & (sub < k + block)
            new = jnp.where(insub | ((lane >= k) & (lane < k + block)), 0.0, a)
            for i in span:
                row = inv[i][0] * right[0]
                for j in range(1, block):
                    row = row + inv[i][j] * right[j]
                col = jnp.broadcast_to(a[:, k + i : k + i + 1], (n, n))
                col = jnp.where(sub == k + i, -1.0, jnp.where(insub, 0.0, col))
                new = new - col * row
            a = new
        a = jnp.concatenate([a[group:], a[:group]], axis=0)
        return pltpu.roll(a, n - group, 1)

    return -lax.fori_loop(0, n // group, sweep, a)


def finish_kernel(
    perms, parent_perm, partial, basis, parent,
    mine, ksend, kin, sibling, wown, win, zout, zin, xout, xin, yout, yin, vout, vin,
    k_s, k_r, s_s, s_r, w_s, w_r, z_s, z_r, x_s, x_r, y_s, y_r, v_s, v_r,
):
    c = lax.axis_index("col")
    zh, x = c // 4, lax.rem(c, 4)
    leaf = partial.shape[1]
    peers = col_peers()
    n = len(peers)
    rank, width = mine.shape
    cut = zout.shape[1]
    tile = 256

    barrier = pltpu.get_barrier_semaphore()
    for j in peers:
        pl.semaphore_signal(barrier, inc=1, device_id={"col": j}, device_id_type=MESH)

    def copy(src, dst, send_sem, recv_sem, j):
        return pltpu.make_async_remote_copy(
            src_ref=src, dst_ref=dst, send_sem=send_sem, recv_sem=recv_sem,
            device_id={"col": j}, device_id_type=MESH,
        )

    lanes = lax.broadcasted_iota(jnp.int32, (rank, leaf), 1)

    def down(row):
        return jnp.broadcast_to(row, (rank, rank)).T[:, :1]

    def pick(j):
        hot = jnp.where(lanes == down(perms[j, 0:1, :]), 1.0, 0.0).astype(BF16)
        return jnp.dot(hot, partial[j], preferred_element_type=F32)

    kc = []
    for i, j in enumerate(peers):
        ksend[i] = pick(j).astype(BF16)
        if i == 0:
            pl.semaphore_wait(barrier, n)
        cp = copy(ksend.at[i], kin.at[i], k_s.at[i], k_r.at[i], j)
        cp.start()
        kc.append(cp)
    total = pick(c)
    for cp in kc:
        cp.wait_recv()
    for i in range(n):
        total = total + kin[i].astype(F32)
    mine[...] = total.astype(BF16)
    to_sibling = copy(mine, sibling, s_s, s_r, c + 1 - 2 * lax.rem(c, 2))
    to_sibling.start()

    skel = mine[...]
    wown[...] = jnp.dot(
        inverse(dot_t(skel, skel)), skel.astype(F32), precision=HI, preferred_element_type=F32
    ).astype(BF16)
    wc = []
    for i, j in enumerate(peers):
        cp = copy(wown, win.at[i], w_s.at[i], w_r.at[i], j)
        cp.start()
        wc.append(cp)

    def times(j, first, last, weight, put):
        def rows(t, carry):
            at = pl.multiple_of(t * tile, tile)
            put(pl.ds(at, tile), dot_t(partial[j, pl.ds(first + at, tile), :], weight[...]))
            return carry

        lax.fori_loop(0, (last - first) // tile, rows, 0)

    def store(ref):
        def put(at, value):
            ref[at, :] = value.astype(ref.dtype)

        return put

    times(c, 0, leaf, wown, store(basis))

    piece = {o: OFFSETS.index(((2 - o[0]) % 2, (4 - o[1]) % 4)) for o in OFFSETS}
    at_x = [lax.rem(x + d, 4) for d in range(4)]
    zpeer = (1 - zh) * 4 + x
    zc, xc = {}, {}
    for d in (2, 1, 3, 0):
        wc[piece[(1, d)]].wait_recv()
        weight = win.at[piece[(1, d)]]
        j = (1 - zh) * 4 + at_x[d]
        times(j, 0, cut, weight, store(zout.at[d]))
        zc[d] = copy(zout.at[d], zin.at[d], z_s.at[d], z_r.at[d], zpeer)
        zc[d].start()
        if d == 0:
            continue
        times(j, cut, leaf, weight, store(xout.at[d - 1, 1]))
        xc[d, 1] = copy(xout.at[d - 1, 1], xin.at[d - 1, 1], x_s.at[d - 1, 1], x_r.at[d - 1, 1], zh * 4 + at_x[d])
        xc[d, 1].start()
        wc[piece[(0, d)]].wait_recv()
        times(zh * 4 + at_x[d], cut, leaf, win.at[piece[(0, d)]], store(xout.at[d - 1, 0]))
        xc[d, 0] = copy(xout.at[d - 1, 0], xin.at[d - 1, 0], x_s.at[d - 1, 0], x_r.at[d - 1, 0], zh * 4 + at_x[d])
        xc[d, 0].start()

    to_sibling.wait()
    odd = lax.rem(c, 2)
    other = sibling[...]
    both = jnp.concatenate([jnp.where(odd == 0, skel, other), jnp.where(odd == 0, other, skel)], axis=0)
    lanes2 = lax.broadcasted_iota(jnp.int32, (rank, 2 * rank), 1)
    order = parent_perm[pl.ds((lax.axis_index("row") * (n + 1) + c) // 2, 1), :]
    hot = jnp.where(lanes2 == down(order[:, :rank]), 1.0, 0.0).astype(BF16)
    chosen = jnp.dot(hot, both, preferred_element_type=F32).astype(BF16)
    parent[...] = jnp.dot(
        dot_t(skel, chosen), inverse(dot_t(chosen, chosen)), precision=HI, preferred_element_type=F32
    )

    yc = {}
    for d in (2, 1, 3):
        zc[d].wait_recv()

        def put(at, value, d=d):
            yout[d - 1, at, :] = (value + zin[d, at, :].astype(F32)).astype(BF16)

        times(zh * 4 + at_x[d], 0, cut, win.at[piece[(0, d)]], put)
        yc[d] = copy(yout.at[d - 1], yin.at[d - 1], y_s.at[d - 1], y_r.at[d - 1], zh * 4 + at_x[d])
        yc[d].start()
        if d == 1:
            for e in (2, 1, 3):
                xc[e, 1].wait_recv()

            def put_v(at, value):
                for e in range(3):
                    value = value + xin[e, 1, at, :].astype(F32)
                vout[at, :] = value.astype(BF16)

            times(zpeer, cut, leaf, win.at[piece[(1, 0)]], put_v)
            vc = copy(vout, vin, v_s, v_r, zpeer)
            vc.start()

    for e in (2, 1, 3):
        xc[e, 0].wait_recv()
    zc[0].wait_recv()
    vc.wait_recv()

    def add_high(t, carry):
        at = pl.multiple_of(t * tile, tile)
        value = basis[pl.ds(cut + at, tile), :] + vin[pl.ds(at, tile), :].astype(F32)
        for e in range(3):
            value = value + xin[e, 0, pl.ds(at, tile), :].astype(F32)
        basis[pl.ds(cut + at, tile), :] = value
        return carry

    lax.fori_loop(0, (leaf - cut) // tile, add_high, 0)
    for d in (2, 1, 3):
        yc[d].wait_recv()

    def add_low(t, carry):
        at = pl.ds(pl.multiple_of(t * tile, tile), tile)
        value = basis[at, :] + zin[0, at, :].astype(F32)
        for e in range(3):
            value = value + yin[e, at, :].astype(F32)
        basis[at, :] = value
        return carry

    lax.fori_loop(0, cut // tile, add_low, 0)
    for cp in kc + wc + list(zc.values()) + list(xc.values()) + list(yc.values()) + [vc]:
        cp.wait_send()


def finish(perms, parent_perm, partial):
    count, _, rank = perms.shape
    leaf, width = partial.shape[1:]
    n = count - 1
    cut = leaf * 5 // 8
    dma = pltpu.SemaphoreType.DMA
    return pl.pallas_call(
        finish_kernel,
        name="finish",
        out_shape=(
            jax.ShapeDtypeStruct((leaf, rank), F32),
            jax.ShapeDtypeStruct((rank, rank), F32),
        ),
        in_specs=[VMEM, VMEM, VMEM],
        out_specs=(VMEM, VMEM),
        scratch_shapes=[
            pltpu.VMEM((rank, width), BF16),
            pltpu.VMEM((n, rank, width), BF16),
            pltpu.VMEM((n, rank, width), BF16),
            pltpu.VMEM((rank, width), BF16),
            pltpu.VMEM((rank, width), BF16),
            pltpu.VMEM((n, rank, width), BF16),
            pltpu.VMEM((4, cut, rank), BF16),
            pltpu.VMEM((4, cut, rank), BF16),
            pltpu.VMEM((3, 2, leaf - cut, rank), BF16),
            pltpu.VMEM((3, 2, leaf - cut, rank), BF16),
            pltpu.VMEM((3, cut, rank), BF16),
            pltpu.VMEM((3, cut, rank), BF16),
            pltpu.VMEM((leaf - cut, rank), BF16),
            pltpu.VMEM((leaf - cut, rank), BF16),
            dma((n,)), dma((n,)), dma, dma, dma((n,)), dma((n,)),
            dma((4,)), dma((4,)), dma((3, 2)), dma((3, 2)), dma((3,)), dma((3,)), dma, dma,
        ],
        compiler_params=pltpu.CompilerParams(
            collective_id=1, has_side_effects=True, vmem_limit_bytes=24 << 20
        ),
    )(perms, parent_perm, partial)


def local(blocks, block_row, block_col, random_cols, leaf_perm, parent_perm):
    n_col = lax.axis_size("col")
    leaf_rows, width = random_cols.shape[2:]
    size = blocks.shape[1]
    rank = parent_perm.shape[1] // 2
    gathered, perms, plan = gather(
        random_cols.reshape(leaf_rows, width), block_row, block_col, leaf_perm[0, :rank]
    )
    partial_value = spmm(plan, blocks, gathered.reshape(-1, size, width), n_col, leaf_rows)
    return finish(perms, parent_perm, partial_value)


def solution(mesh):
    in_specs = (
        P(("row", "col"), None, None),
        P(("row", "col")),
        P(("row", "col")),
        P("col", "row", None, None),
        P(("row", "col"), None),
        P(),
    )
    out_specs = (P(("row", "col"), None), P(("row", "col"), None))
    return jax.shard_map(local, mesh=mesh, in_specs=in_specs, out_specs=out_specs, check_vma=False)
```

```python
import functools

import jax
import jax.numpy as jnp
from jax import lax
from jax.experimental import pallas as pl
from jax.experimental.pallas import tpu as pltpu
from jax.sharding import PartitionSpec as P

HI = lax.Precision.HIGHEST
VMEM = pl.BlockSpec(memory_space=pltpu.VMEM)
SMEM = pl.BlockSpec(memory_space=pltpu.SMEM)
HBM = pl.BlockSpec(memory_space=pltpu.HBM)
F32 = jnp.float32
BF16 = jnp.bfloat16


def schedule(rows, cols):
    count, lanes = rows.shape[1], 128
    nrows, steps = 128, 256

    def iota(shape, dim):
        return lax.broadcasted_iota(jnp.int32, shape, dim)

    def ones(mask):
        return jnp.where(mask, 1, 0)

    def down(value):
        return jnp.broadcast_to(value, (lanes, count)).T

    rows_k, cols_k = down(rows), down(cols)
    lane = iota((count, lanes), 1)
    sub = iota((count, lanes), 0)
    within = jnp.zeros((count, 1), jnp.int32)
    for part in range(count // lanes):
        other = jnp.broadcast_to(rows[:, part * lanes : (part + 1) * lanes], (count, lanes))
        same = (other == rows_k) & (lane + part * lanes < sub)
        within = within + jnp.sum(ones(same), axis=1, keepdims=True)
    held = jnp.sum(ones(rows_k == lane), axis=0, keepdims=True)
    pairs = lax.shift_right_logical(held + 1, 1)
    base = jnp.sum(jnp.where(lane < rows_k, jnp.broadcast_to(pairs, (count, lanes)), 0), axis=1, keepdims=True)
    place = jnp.broadcast_to(2 * base + within, (count, lanes))
    code = (sub + 1) * 65536 + cols_k
    lane_r, sub_r = iota((nrows, lanes), 1), iota((nrows, lanes), 0)
    pairs_all = jnp.broadcast_to(pairs, (nrows, lanes))
    before = jnp.broadcast_to(
        jnp.sum(jnp.where(lane_r < sub_r, pairs_all, 0), axis=1, keepdims=True), (nrows, lanes)
    )
    end = before + jnp.broadcast_to(
        jnp.sum(jnp.where(lane_r == sub_r, pairs_all, 0), axis=1, keepdims=True), (nrows, lanes)
    )
    out = []
    for part in range(2 * steps // lanes):
        out.append(jnp.sum(jnp.where(place == lane + part * lanes, code, 0), axis=0, keepdims=True))
    for part in range(steps // lanes):
        q = lane_r + part * lanes
        row = jnp.minimum(jnp.sum(ones(end <= q), axis=0, keepdims=True), nrows - 1)
        out.append(2 * row + jnp.sum(ones(before == q), axis=0, keepdims=True))
    total = jnp.sum(jnp.where(sub_r == 0, jnp.broadcast_to(jnp.max(end, axis=0, keepdims=True), (nrows, lanes)), 0), axis=0, keepdims=True)
    return out + [total, jnp.zeros_like(total)]


MESH = pl.DeviceIdType.MESH


OFFSETS = ((1, 2), (0, 2), (1, 1), (1, 3), (0, 1), (0, 3), (1, 0))


def col_peers():
    c = lax.axis_index("col")
    zh, x = c // 4, lax.rem(c, 4)
    return [lax.rem(zh + dz, 2) * 4 + lax.rem(x + dx, 4) for dz, dx in OFFSETS]


def gather_kernel(
    own, ints, out, perms, plan,
    perm, local_sem, send_sem, recv_sem, core_send, core_recv, perm_local, perm_send, perm_recv,
):
    r = lax.axis_index("row")
    y, zl, co = r // 4, lax.rem(r // 2, 2), lax.rem(r, 2)
    size = own.shape[0]
    half = size // 2
    low = size * 7 // 16
    mid = low + (size - low) // 2

    def at(dy, dz, dc=0):
        return lax.rem(y + dy + 4, 4) * 4 + lax.rem(zl + dz, 2) * 2 + lax.rem(co + dc, 2)

    up, down, side, core = at(1, 0), at(-1, 0), at(0, 1), at(0, 0, 1)
    barrier = pltpu.get_barrier_semaphore()
    for peer in (up, down, side, core):
        pl.semaphore_signal(barrier, inc=1, device_id={"row": peer}, device_id_type=MESH)
    peers = col_peers()
    for j in peers:
        pl.semaphore_signal(barrier, inc=1, device_id={"col": j}, device_id_type=MESH)
    keep = pltpu.make_async_copy(own, out.at[pl.ds(pl.multiple_of(r * size, size), size)], local_sem)
    keep.start()
    n_blocks = (ints.shape[1] - size) // 2
    perm[...] = jnp.broadcast_to(ints[:, 2 * n_blocks : 2 * n_blocks + perm.shape[1]], perm.shape)
    keep_perm = pltpu.make_async_copy(perm, perms.at[lax.axis_index("col")], perm_local)
    keep_perm.start()
    pl.semaphore_wait(barrier, 4 + len(peers))

    def rows(source, first, last):
        return pl.ds(pl.multiple_of(source * size + first, 16), last - first)

    sent = []

    def send(source, first, last, target, slot, mine=False):
        dst = out.at[rows(source, first, last)]
        cp = pltpu.make_async_remote_copy(
            src_ref=own.at[pl.ds(first, last - first)] if mine else dst,
            dst_ref=dst,
            send_sem=send_sem.at[len(sent)],
            recv_sem=recv_sem.at[slot],
            device_id={"row": target},
            device_id_type=MESH,
        )
        cp.start()
        sent.append(cp)
        return cp

    crossed = []

    def cross(source, first, last, mine=False):
        dst = out.at[rows(source, first, last)]
        cp = pltpu.make_async_remote_copy(
            src_ref=own if mine else dst,
            dst_ref=dst,
            send_sem=core_send.at[len(crossed)],
            recv_sem=core_recv.at[len(crossed)],
            device_id={"row": core},
            device_id_type=MESH,
        )
        cp.start()
        crossed.append(cp)

    def arrived(source, first, last, slot):
        dst = out.at[rows(source, first, last)]
        pltpu.make_async_remote_copy(
            src_ref=dst,
            dst_ref=dst,
            send_sem=send_sem.at[0],
            recv_sem=recv_sem.at[slot],
            device_id={"row": core},
            device_id_type=MESH,
        ).wait_recv()

    send(r, 0, half, up, 0, True)
    send(r, half, size, down, 2, True)
    send(r, low, size, side, 4, True)
    send(r, half, size, up, 1, True)
    send(r, 0, half, down, 3, True)
    send(r, 0, low, side, 5, True)
    cross(r, 0, size, True)
    orders = []
    for i, j in enumerate(peers):
        cp = pltpu.make_async_remote_copy(
            src_ref=perm,
            dst_ref=perms.at[lax.axis_index("col")],
            send_sem=perm_send.at[i],
            recv_sem=perm_recv.at[i],
            device_id={"col": j},
            device_id_type=MESH,
        )
        cp.start()
        orders.append(cp)
    for i, value in enumerate(schedule(ints[:, :n_blocks], ints[:, n_blocks : 2 * n_blocks])):
        plan[i : i + 1, :] = value

    prev, nxt, far = at(-1, 0), at(1, 0), at(2, 0)
    zown, zprev, znext, zfar = at(0, 1), at(-1, 1), at(1, 1), at(2, 1)

    arrived(prev, 0, half, 0)
    far_up = send(prev, 0, half, up, 6)
    send(prev, 0, low, side, 10)
    cross(prev, 0, half)
    arrived(nxt, half, size, 2)
    far_down = send(nxt, half, size, down, 7)
    cross(nxt, half, size)
    arrived(nxt, 0, half, 3)
    send(nxt, 0, low, side, 11)
    cross(nxt, 0, half)
    arrived(prev, half, size, 1)
    cross(prev, half, size)
    arrived(zown, low, size, 4)
    cross(zown, low, size)
    arrived(zown, 0, low, 5)
    cross(zown, 0, low)
    far_up.wait_send()
    send(zown, low, size, up, 8)
    far_down.wait_send()
    send(zown, low, size, down, 9)
    arrived(far, 0, half, 6)
    send(far, 0, low, side, 14)
    cross(far, 0, half)
    arrived(far, half, size, 7)
    cross(far, half, size)
    arrived(zprev, low, size, 8)
    send(zprev, low, mid, up, 12)
    cross(zprev, low, size)
    arrived(znext, low, size, 9)
    send(znext, mid, size, down, 13)
    cross(znext, low, size)
    arrived(zprev, 0, low, 10)
    cross(zprev, 0, low)
    arrived(znext, 0, low, 11)
    cross(znext, 0, low)
    arrived(zfar, low, mid, 12)
    cross(zfar, low, mid)
    arrived(zfar, mid, size, 13)
    cross(zfar, mid, size)
    arrived(zfar, 0, low, 14)
    cross(zfar, 0, low)
    keep.wait()
    keep_perm.wait()
    for cp in orders:
        cp.wait()
    for cp in sent:
        if cp is not far_up and cp is not far_down:
            cp.wait_send()
    for cp in crossed:
        cp.wait()


def gather(own, rows, cols, order, rank):
    size, width = own.shape
    count, n_col = lax.axis_size("row"), lax.axis_size("col")
    ints = jnp.concatenate([rows, cols, order])[None, :]
    dma = pltpu.SemaphoreType.DMA
    return pl.pallas_call(
        gather_kernel,
        name="gather",
        out_shape=(
            jax.ShapeDtypeStruct((count * size, width), own.dtype),
            jax.ShapeDtypeStruct((n_col, 8, rank), jnp.int32),
            jax.ShapeDtypeStruct((8, 128), jnp.int32),
        ),
        in_specs=[HBM, VMEM],
        out_specs=(HBM, HBM, VMEM),
        scratch_shapes=[
            pltpu.VMEM((8, rank), jnp.int32),
            dma, dma((16,)), dma((15,)), dma((16,)), dma((16,)), dma, dma((n_col - 1,)), dma((n_col - 1,)),
        ],
        compiler_params=pltpu.CompilerParams(
            collective_id=0, has_side_effects=True, vmem_limit_bytes=4 << 20
        ),
        cost_estimate=pl.CostEstimate(flops=60000000000, bytes_accessed=40000000, transcendentals=0),
    )(own, ints)


UNROLL = 8


def spmm_kernel(plan, blocks, rand, out, acc):
    acc[...] = jnp.zeros_like(acc)
    size = acc.shape[0]
    per = out.shape[1] // size

    def pair(q):
        mats, rights = [], []
        for s in range(2):
            t = 2 * q + s
            code = plan[t // 128, lax.rem(t, 128)]
            k = jnp.maximum(lax.shift_right_logical(code, 16) - 1, 0)
            col = jnp.bitwise_and(code, 65535)
            mat = blocks[k]
            mats.append(jnp.where(code > 0, mat, jnp.zeros_like(mat)))
            rights.append(rand[col])
        return jnp.dot(
            jnp.concatenate(mats, axis=1),
            jnp.concatenate(rights, axis=0),
            preferred_element_type=F32,
        )

    def body(g, carry):
        prods = [pair(g * UNROLL + u) for u in range(UNROLL)]
        for u in range(UNROLL):
            q = g * UNROLL + u
            info = plan[4 + q // 128, lax.rem(q, 128)]
            keep = (1 - jnp.bitwise_and(info, 1)).astype(F32)
            value = acc[...] * keep + prods[u]
            acc[...] = value
            row = lax.shift_right_logical(info, 1)
            at = pl.multiple_of(lax.rem(row, per) * size, size)
            out[row // per, pl.ds(at, size), :] = value.astype(BF16)
        return carry

    lax.fori_loop(0, (plan[6, 0] + UNROLL - 1) // UNROLL, body, 0)


def spmm(plan, blocks, rand, leaves, leaf_rows):
    size, width = blocks.shape[1], rand.shape[2]
    return pl.pallas_call(
        spmm_kernel,
        name="spmm",
        out_shape=jax.ShapeDtypeStruct((leaves, leaf_rows, width), BF16),
        in_specs=[SMEM, VMEM, VMEM],
        out_specs=VMEM,
        scratch_shapes=[pltpu.VMEM((size, width), F32)],
        compiler_params=pltpu.CompilerParams(vmem_limit_bytes=4 << 20),
    )(plan, blocks, rand)


def dot_t(a, b):
    return lax.dot_general(a, b, (((1,), (1,)), ((), ())), preferred_element_type=F32)


def inverse_small(d):
    r = 1.0 / (d[0][0] * d[1][1] - d[0][1] * d[0][1])
    a00, a01, a11 = d[1][1] * r, -d[0][1] * r, d[0][0] * r
    x = [[a00 * d[0][2 + j] + a01 * d[1][2 + j] for j in range(2)], [a01 * d[0][2 + j] + a11 * d[1][2 + j] for j in range(2)]]
    s00 = d[2][2] - (d[0][2] * x[0][0] + d[1][2] * x[1][0])
    s01 = d[2][3] - (d[0][2] * x[0][1] + d[1][2] * x[1][1])
    s11 = d[3][3] - (d[0][3] * x[0][1] + d[1][3] * x[1][1])
    q = 1.0 / (s00 * s11 - s01 * s01)
    c00, c01, c11 = s11 * q, -s01 * q, s00 * q
    y = [[x[i][0] * c00 + x[i][1] * c01, x[i][0] * c01 + x[i][1] * c11] for i in range(2)]
    t00 = a00 + y[0][0] * x[0][0] + y[0][1] * x[0][1]
    t01 = a01 + y[0][0] * x[1][0] + y[0][1] * x[1][1]
    t11 = a11 + y[1][0] * x[1][0] + y[1][1] * x[1][1]
    return [
        [t00, t01, -y[0][0], -y[0][1]],
        [t01, t11, -y[1][0], -y[1][1]],
        [-y[0][0], -y[1][0], c00, c01],
        [-y[0][1], -y[1][1], c01, c11],
    ]


def inverse(a):
    n = a.shape[0]
    group, block = 8, 4
    lane = lax.broadcasted_iota(jnp.int32, (n, n), 1)
    sub = lax.broadcasted_iota(jnp.int32, (n, n), 0)
    lane1 = lax.broadcasted_iota(jnp.int32, (1, n), 1)

    def sweep(g, a):
        for k in range(0, group, block):
            span = range(block)
            d = [[None] * block for _ in span]
            for i in span:
                for j in range(i, block):
                    d[i][j] = jnp.broadcast_to(a[k + i : k + i + 1, k + j : k + j + 1], (1, n))
            inv = inverse_small(d)
            inside1 = (lane1 >= k) & (lane1 < k + block)
            right = [
                jnp.where(lane1 == k + j, -1.0, jnp.where(inside1, 0.0, a[k + j : k + j + 1, :])) for j in span
            ]
            insub = (sub >= k) & (sub < k + block)
            new = jnp.where(insub | ((lane >= k) & (lane < k + block)), 0.0, a)
            for i in span:
                row = inv[i][0] * right[0]
                for j in range(1, block):
                    row = row + inv[i][j] * right[j]
                col = jnp.broadcast_to(a[:, k + i : k + i + 1], (n, n))
                col = jnp.where(sub == k + i, -1.0, jnp.where(insub, 0.0, col))
                new = new - col * row
            a = new
        a = jnp.concatenate([a[group:], a[:group]], axis=0)
        return pltpu.roll(a, n - group, 1)

    return -lax.fori_loop(0, n // group, sweep, a)


def finish_kernel(
    perms, parent_perm, partial, basis, parent,
    mine, ksend, kin, sibling, wown, win, zout, zin, xout, xin, yout, yin, vout, vin, rzin, rxin,
    k_s, k_r, s_s, s_r, w_s, w_r, z_s, z_r, x_s, x_r, y_s, y_r, v_s, v_r, rz_s, rz_r, rx_s, rx_r,
):
    c = lax.axis_index("col")
    zh, x = c // 4, lax.rem(c, 4)
    leaf = partial.shape[1]
    peers = col_peers()
    n = len(peers)
    rank, width = mine.shape
    cut, raw = zout.shape[1], rzin.shape[1]
    top, last = leaf - 2 * raw, leaf - raw
    tile = 128

    barrier = pltpu.get_barrier_semaphore()
    for j in peers:
        pl.semaphore_signal(barrier, inc=1, device_id={"col": j}, device_id_type=MESH)

    def copy(src, dst, send_sem, recv_sem, j):
        return pltpu.make_async_remote_copy(
            src_ref=src, dst_ref=dst, send_sem=send_sem, recv_sem=recv_sem,
            device_id={"col": j}, device_id_type=MESH,
        )

    lanes = lax.broadcasted_iota(jnp.int32, (rank, leaf), 1)

    def down(row):
        return jnp.broadcast_to(row, (rank, rank)).T[:, :1]

    def pick(j):
        hot = jnp.where(lanes == down(perms[j, 0:1, :]), 1.0, 0.0).astype(BF16)
        return jnp.dot(hot, partial[j], preferred_element_type=F32)

    kc = []
    for i, j in enumerate(peers):
        ksend[i] = pick(j).astype(BF16)
        if i == 0:
            pl.semaphore_wait(barrier, n)
        cp = copy(ksend.at[i], kin.at[i], k_s.at[i], k_r.at[i], j)
        cp.start()
        kc.append(cp)
    total = pick(c)
    for cp in kc:
        cp.wait_recv()
    for i in range(n):
        total = total + kin[i].astype(F32)
    mine[...] = total.astype(BF16)
    to_sibling = copy(mine, sibling, s_s, s_r, c + 1 - 2 * lax.rem(c, 2))
    to_sibling.start()
    at_x = [lax.rem(x + d, 4) for d in range(4)]
    zpeer = (1 - zh) * 4 + x
    rz, rx = {}, {}
    for d in (2, 1, 3, 0):
        rz[d] = copy(
            partial.at[(1 - zh) * 4 + at_x[d], pl.ds(top, raw)], rzin.at[d], rz_s.at[d], rz_r.at[d], zpeer
        )
        rz[d].start()
        if d == 0:
            continue
        for h in range(2):
            rx[d, h] = copy(
                partial.at[lax.rem(zh + h, 2) * 4 + at_x[d], pl.ds(last, raw)],
                rxin.at[d - 1, h], rx_s.at[d - 1, h], rx_r.at[d - 1, h], zh * 4 + at_x[d],
            )
            rx[d, h].start()

    skel = mine[...]
    wown[...] = jnp.dot(
        inverse(dot_t(skel, skel)), skel.astype(F32), precision=HI, preferred_element_type=F32
    ).astype(BF16)
    wc = []
    for i, j in enumerate(peers):
        cp = copy(wown, win.at[i], w_s.at[i], w_r.at[i], j)
        cp.start()
        wc.append(cp)

    def times(j, first, last, weight, put):
        value = dot_t(partial[j, pl.ds(first, last - first), :], weight[...])
        put(pl.ds(0, last - first), value)

    def store(ref):
        def put(at, value):
            ref[at, :] = value.astype(ref.dtype)

        return put

    times(c, 0, top, wown, store(basis))

    piece = {o: OFFSETS.index(((2 - o[0]) % 2, (4 - o[1]) % 4)) for o in OFFSETS}
    zc, xc = {}, {}
    for d in (2, 1, 3, 0):
        wc[piece[(1, d)]].wait_recv()
        weight = win.at[piece[(1, d)]]
        j = (1 - zh) * 4 + at_x[d]
        times(j, 0, cut, weight, store(zout.at[d]))
        zc[d] = copy(zout.at[d], zin.at[d], z_s.at[d], z_r.at[d], zpeer)
        zc[d].start()
        if d == 0:
            continue
        times(j, cut, top, weight, store(xout.at[d - 1, 1]))
        xc[d, 1] = copy(xout.at[d - 1, 1], xin.at[d - 1, 1], x_s.at[d - 1, 1], x_r.at[d - 1, 1], zh * 4 + at_x[d])
        xc[d, 1].start()
        wc[piece[(0, d)]].wait_recv()
        times(zh * 4 + at_x[d], cut, top, win.at[piece[(0, d)]], store(xout.at[d - 1, 0]))
        xc[d, 0] = copy(xout.at[d - 1, 0], xin.at[d - 1, 0], x_s.at[d - 1, 0], x_r.at[d - 1, 0], zh * 4 + at_x[d])
        xc[d, 0].start()

    to_sibling.wait()
    odd = lax.rem(c, 2)
    other = sibling[...]
    both = jnp.concatenate([jnp.where(odd == 0, skel, other), jnp.where(odd == 0, other, skel)], axis=0)
    lanes2 = lax.broadcasted_iota(jnp.int32, (rank, 2 * rank), 1)
    order = parent_perm[pl.ds((lax.axis_index("row") * (n + 1) + c) // 2, 1), :]
    hot = jnp.where(lanes2 == down(order[:, :rank]), 1.0, 0.0).astype(BF16)
    chosen = jnp.dot(hot, both, preferred_element_type=F32).astype(BF16)
    parent[...] = jnp.dot(
        dot_t(skel, chosen), inverse(dot_t(chosen, chosen)), precision=HI, preferred_element_type=F32
    )

    def over_z(d):
        rz[d].wait_recv()
        return (partial[zh * 4 + at_x[d], pl.ds(top, raw), :].astype(F32) + rzin[d].astype(F32)).astype(BF16)

    def over_x(h):
        for e in (2, 1, 3):
            rx[e, h].wait_recv()
        value = partial[lax.rem(zh + h, 2) * 4 + x, pl.ds(last, raw), :].astype(F32)
        for e in range(3):
            value = value + rxin[e, h].astype(F32)
        return value.astype(BF16)

    yc = {}
    for d in (2, 1, 3):
        zc[d].wait_recv()

        def put(at, value, d=d):
            yout[d - 1, at, :] = (value + zin[d, at, :].astype(F32)).astype(BF16)

        times(zh * 4 + at_x[d], 0, cut, win.at[piece[(0, d)]], put)
        yout[d - 1, pl.ds(cut, raw), :] = dot_t(over_z(d), win[piece[(0, d)]]).astype(BF16)
        yc[d] = copy(yout.at[d - 1], yin.at[d - 1], y_s.at[d - 1], y_r.at[d - 1], zh * 4 + at_x[d])
        yc[d].start()
        if d == 1:
            for e in (2, 1, 3):
                xc[e, 1].wait_recv()

            def put_v(at, value):
                for e in range(3):
                    value = value + xin[e, 1, at, :].astype(F32)
                vout[at, :] = value.astype(BF16)

            times(zpeer, cut, top, win.at[piece[(1, 0)]], put_v)
            vout[pl.ds(top - cut, raw), :] = dot_t(over_x(1), win[piece[(1, 0)]]).astype(BF16)
            vc = copy(vout, vin, v_s, v_r, zpeer)
            vc.start()

    basis[pl.ds(top, raw), :] = dot_t(over_z(0), wown[...])
    basis[pl.ds(last, raw), :] = dot_t(over_x(0), wown[...])
    for e in (2, 1, 3):
        xc[e, 0].wait_recv()
    zc[0].wait_recv()
    vc.wait_recv()

    def add_high(t, carry):
        at = pl.multiple_of(t * tile, tile)
        value = basis[pl.ds(cut + at, tile), :] + vin[pl.ds(at, tile), :].astype(F32)
        for e in range(3):
            value = value + xin[e, 0, pl.ds(at, tile), :].astype(F32)
        basis[pl.ds(cut + at, tile), :] = value
        return carry

    lax.fori_loop(0, (top - cut) // tile, add_high, 0)
    basis[pl.ds(last, raw), :] = basis[pl.ds(last, raw), :] + vin[pl.ds(top - cut, raw), :].astype(F32)
    for d in (2, 1, 3):
        yc[d].wait_recv()

    def add_low(t, carry):
        at = pl.ds(pl.multiple_of(t * tile, tile), tile)
        value = basis[at, :] + zin[0, at, :].astype(F32)
        for e in range(3):
            value = value + yin[e, at, :].astype(F32)
        basis[at, :] = value
        return carry

    lax.fori_loop(0, cut // tile, add_low, 0)
    value = basis[pl.ds(top, raw), :]
    for e in range(3):
        value = value + yin[e, pl.ds(cut, raw), :].astype(F32)
    basis[pl.ds(top, raw), :] = value
    for cp in kc + wc + list(zc.values()) + list(xc.values()) + list(yc.values()) + list(rz.values()) + list(rx.values()) + [vc]:
        cp.wait_send()


def finish(perms, parent_perm, partial):
    count, _, rank = perms.shape
    leaf, width = partial.shape[1:]
    n = count - 1
    raw = leaf // 16
    cut = leaf * 9 // 16
    dma = pltpu.SemaphoreType.DMA
    return pl.pallas_call(
        finish_kernel,
        name="finish",
        out_shape=(
            jax.ShapeDtypeStruct((leaf, rank), F32),
            jax.ShapeDtypeStruct((rank, rank), F32),
        ),
        in_specs=[VMEM, VMEM, VMEM],
        out_specs=(VMEM, VMEM),
        scratch_shapes=[
            pltpu.VMEM((rank, width), BF16),
            pltpu.VMEM((n, rank, width), BF16),
            pltpu.VMEM((n, rank, width), BF16),
            pltpu.VMEM((rank, width), BF16),
            pltpu.VMEM((rank, width), BF16),
            pltpu.VMEM((n, rank, width), BF16),
            pltpu.VMEM((4, cut, rank), BF16),
            pltpu.VMEM((4, cut, rank), BF16),
            pltpu.VMEM((3, 2, leaf - cut - 2 * raw, rank), BF16),
            pltpu.VMEM((3, 2, leaf - cut - 2 * raw, rank), BF16),
            pltpu.VMEM((3, cut + raw, rank), BF16),
            pltpu.VMEM((3, cut + raw, rank), BF16),
            pltpu.VMEM((leaf - cut - raw, rank), BF16),
            pltpu.VMEM((leaf - cut - raw, rank), BF16),
            pltpu.VMEM((4, raw, width), BF16),
            pltpu.VMEM((3, 2, raw, width), BF16),
            dma((n,)), dma((n,)), dma, dma, dma((n,)), dma((n,)),
            dma((4,)), dma((4,)), dma((3, 2)), dma((3, 2)), dma((3,)), dma((3,)), dma, dma,
            dma((4,)), dma((4,)), dma((3, 2)), dma((3, 2)),
        ],
        compiler_params=pltpu.CompilerParams(
            collective_id=1, has_side_effects=True, vmem_limit_bytes=24 << 20
        ),
    )(perms, parent_perm, partial)


def local(blocks, block_row, block_col, random_cols, leaf_perm, parent_perm):
    n_col = lax.axis_size("col")
    leaf_rows, width = random_cols.shape[2:]
    size = blocks.shape[1]
    rank = parent_perm.shape[1] // 2
    gathered, perms, plan = gather(
        random_cols.reshape(leaf_rows, width), block_row, block_col, leaf_perm.reshape(-1), rank
    )
    partial_value = spmm(plan, blocks, gathered.reshape(-1, size, width), n_col, leaf_rows)
    return finish(perms, parent_perm, partial_value)


def solution(mesh):
    in_specs = (
        P(("row", "col"), None, None),
        P(("row", "col")),
        P(("row", "col")),
        P("col", "row", None, None),
        P(("row", "col"), None),
        P(),
    )
    out_specs = (P(("row", "col"), None), P(("row", "col"), None))
    return jax.shard_map(local, mesh=mesh, in_specs=in_specs, out_specs=out_specs, check_vma=False)
```

```python
import functools

import jax
import jax.numpy as jnp
from jax import lax
from jax.experimental import pallas as pl
from jax.experimental.pallas import tpu as pltpu
from jax.sharding import PartitionSpec as P

HI = lax.Precision.HIGHEST
VMEM = pl.BlockSpec(memory_space=pltpu.VMEM)
SMEM = pl.BlockSpec(memory_space=pltpu.SMEM)
HBM = pl.BlockSpec(memory_space=pltpu.HBM)
F32 = jnp.float32
BF16 = jnp.bfloat16


def schedule(rows, cols):
    count, lanes = rows.shape[1], 128
    nrows, steps = 128, 256

    def iota(shape, dim):
        return lax.broadcasted_iota(jnp.int32, shape, dim)

    def ones(mask):
        return jnp.where(mask, 1, 0)

    def down(value):
        return jnp.broadcast_to(value, (lanes, count)).T

    rows_k, cols_k = down(rows), down(cols)
    lane = iota((count, lanes), 1)
    sub = iota((count, lanes), 0)
    within = jnp.zeros((count, 1), jnp.int32)
    for part in range(count // lanes):
        other = jnp.broadcast_to(rows[:, part * lanes : (part + 1) * lanes], (count, lanes))
        same = (other == rows_k) & (lane + part * lanes < sub)
        within = within + jnp.sum(ones(same), axis=1, keepdims=True)
    held = jnp.sum(ones(rows_k == lane), axis=0, keepdims=True)
    pairs = lax.shift_right_logical(held + 1, 1)
    base = jnp.sum(jnp.where(lane < rows_k, jnp.broadcast_to(pairs, (count, lanes)), 0), axis=1, keepdims=True)
    place = jnp.broadcast_to(2 * base + within, (count, lanes))
    code = (sub + 1) * 65536 + cols_k
    lane_r, sub_r = iota((nrows, lanes), 1), iota((nrows, lanes), 0)
    pairs_all = jnp.broadcast_to(pairs, (nrows, lanes))
    before = jnp.broadcast_to(
        jnp.sum(jnp.where(lane_r < sub_r, pairs_all, 0), axis=1, keepdims=True), (nrows, lanes)
    )
    end = before + jnp.broadcast_to(
        jnp.sum(jnp.where(lane_r == sub_r, pairs_all, 0), axis=1, keepdims=True), (nrows, lanes)
    )
    out = []
    for part in range(2 * steps // lanes):
        out.append(jnp.sum(jnp.where(place == lane + part * lanes, code, 0), axis=0, keepdims=True))
    for part in range(steps // lanes):
        q = lane_r + part * lanes
        row = jnp.minimum(jnp.sum(ones(end <= q), axis=0, keepdims=True), nrows - 1)
        out.append(2 * row + jnp.sum(ones(before == q), axis=0, keepdims=True))
    total = jnp.sum(jnp.where(sub_r == 0, jnp.broadcast_to(jnp.max(end, axis=0, keepdims=True), (nrows, lanes)), 0), axis=0, keepdims=True)
    return out + [total, jnp.zeros_like(total)]


MESH = pl.DeviceIdType.MESH


OFFSETS = ((1, 2), (0, 2), (1, 1), (1, 3), (0, 1), (0, 3), (1, 0))


def col_peers():
    c = lax.axis_index("col")
    zh, x = c // 4, lax.rem(c, 4)
    return [lax.rem(zh + dz, 2) * 4 + lax.rem(x + dx, 4) for dz, dx in OFFSETS]


def gather_kernel(
    own, ints, out, perms, plan,
    perm, local_sem, send_sem, recv_sem, core_send, core_recv, perm_local, perm_send, perm_recv,
):
    r = lax.axis_index("row")
    y, zl, co = r // 4, lax.rem(r // 2, 2), lax.rem(r, 2)
    size = own.shape[0]
    half = size // 2
    low = size * 7 // 16
    mid = low + (size - low) // 2

    def at(dy, dz, dc=0):
        return lax.rem(y + dy + 4, 4) * 4 + lax.rem(zl + dz, 2) * 2 + lax.rem(co + dc, 2)

    up, down, side, core = at(1, 0), at(-1, 0), at(0, 1), at(0, 0, 1)
    barrier = pltpu.get_barrier_semaphore()
    for peer in (up, down, side, core):
        pl.semaphore_signal(barrier, inc=1, device_id={"row": peer}, device_id_type=MESH)
    peers = col_peers()
    for j in peers:
        pl.semaphore_signal(barrier, inc=1, device_id={"col": j}, device_id_type=MESH)
    keep = pltpu.make_async_copy(own, out.at[pl.ds(pl.multiple_of(r * size, size), size)], local_sem)
    keep.start()
    n_blocks = (ints.shape[1] - size) // 2
    perm[...] = jnp.broadcast_to(ints[:, 2 * n_blocks : 2 * n_blocks + perm.shape[1]], perm.shape)
    keep_perm = pltpu.make_async_copy(perm, perms.at[lax.axis_index("col")], perm_local)
    keep_perm.start()
    pl.semaphore_wait(barrier, 4 + len(peers))

    def rows(source, first, last):
        return pl.ds(pl.multiple_of(source * size + first, 16), last - first)

    sent = []

    def send(source, first, last, target, slot, mine=False):
        dst = out.at[rows(source, first, last)]
        cp = pltpu.make_async_remote_copy(
            src_ref=own.at[pl.ds(first, last - first)] if mine else dst,
            dst_ref=dst,
            send_sem=send_sem.at[len(sent)],
            recv_sem=recv_sem.at[slot],
            device_id={"row": target},
            device_id_type=MESH,
        )
        cp.start()
        sent.append(cp)
        return cp

    crossed = []

    def cross(source, first, last, mine=False):
        dst = out.at[rows(source, first, last)]
        cp = pltpu.make_async_remote_copy(
            src_ref=own if mine else dst,
            dst_ref=dst,
            send_sem=core_send.at[len(crossed)],
            recv_sem=core_recv.at[len(crossed)],
            device_id={"row": core},
            device_id_type=MESH,
        )
        cp.start()
        crossed.append(cp)

    def arrived(source, first, last, slot):
        dst = out.at[rows(source, first, last)]
        pltpu.make_async_remote_copy(
            src_ref=dst,
            dst_ref=dst,
            send_sem=send_sem.at[0],
            recv_sem=recv_sem.at[slot],
            device_id={"row": core},
            device_id_type=MESH,
        ).wait_recv()

    send(r, 0, half, up, 0, True)
    send(r, half, size, down, 2, True)
    send(r, low, size, side, 4, True)
    send(r, half, size, up, 1, True)
    send(r, 0, half, down, 3, True)
    send(r, 0, low, side, 5, True)
    cross(r, 0, size, True)
    orders = []
    for i, j in enumerate(peers):
        cp = pltpu.make_async_remote_copy(
            src_ref=perm,
            dst_ref=perms.at[lax.axis_index("col")],
            send_sem=perm_send.at[i],
            recv_sem=perm_recv.at[i],
            device_id={"col": j},
            device_id_type=MESH,
        )
        cp.start()
        orders.append(cp)
    for i, value in enumerate(schedule(ints[:, :n_blocks], ints[:, n_blocks : 2 * n_blocks])):
        plan[i : i + 1, :] = value

    prev, nxt, far = at(-1, 0), at(1, 0), at(2, 0)
    zown, zprev, znext, zfar = at(0, 1), at(-1, 1), at(1, 1), at(2, 1)

    arrived(prev, 0, half, 0)
    far_up = send(prev, 0, half, up, 6)
    send(prev, 0, low, side, 10)
    cross(prev, 0, half)
    arrived(nxt, half, size, 2)
    far_down = send(nxt, half, size, down, 7)
    cross(nxt, half, size)
    arrived(nxt, 0, half, 3)
    send(nxt, 0, low, side, 11)
    cross(nxt, 0, half)
    arrived(prev, half, size, 1)
    cross(prev, half, size)
    arrived(zown, low, size, 4)
    cross(zown, low, size)
    arrived(zown, 0, low, 5)
    cross(zown, 0, low)
    far_up.wait_send()
    send(zown, low, size, up, 8)
    far_down.wait_send()
    send(zown, low, size, down, 9)
    arrived(far, 0, half, 6)
    send(far, 0, low, side, 14)
    cross(far, 0, half)
    arrived(far, half, size, 7)
    cross(far, half, size)
    arrived(zprev, low, size, 8)
    send(zprev, low, mid, up, 12)
    cross(zprev, low, size)
    arrived(znext, low, size, 9)
    send(znext, mid, size, down, 13)
    cross(znext, low, size)
    arrived(zprev, 0, low, 10)
    cross(zprev, 0, low)
    arrived(znext, 0, low, 11)
    cross(znext, 0, low)
    arrived(zfar, low, mid, 12)
    cross(zfar, low, mid)
    arrived(zfar, mid, size, 13)
    cross(zfar, mid, size)
    arrived(zfar, 0, low, 14)
    cross(zfar, 0, low)
    keep.wait()
    keep_perm.wait()
    for cp in orders:
        cp.wait()
    for cp in sent:
        if cp is not far_up and cp is not far_down:
            cp.wait_send()
    for cp in crossed:
        cp.wait()


def gather(own, rows, cols, order, rank):
    size, width = own.shape
    count, n_col = lax.axis_size("row"), lax.axis_size("col")
    ints = jnp.concatenate([rows, cols, order])[None, :]
    dma = pltpu.SemaphoreType.DMA
    return pl.pallas_call(
        gather_kernel,
        name="gather",
        out_shape=(
            jax.ShapeDtypeStruct((count * size, width), own.dtype),
            jax.ShapeDtypeStruct((n_col, 8, rank), jnp.int32),
            jax.ShapeDtypeStruct((8, 128), jnp.int32),
        ),
        in_specs=[HBM, VMEM],
        out_specs=(HBM, HBM, VMEM),
        scratch_shapes=[
            pltpu.VMEM((8, rank), jnp.int32),
            dma, dma((16,)), dma((15,)), dma((16,)), dma((16,)), dma, dma((n_col - 1,)), dma((n_col - 1,)),
        ],
        compiler_params=pltpu.CompilerParams(
            collective_id=0, has_side_effects=True, vmem_limit_bytes=4 << 20
        ),
        cost_estimate=pl.CostEstimate(flops=60000000000, bytes_accessed=40000000, transcendentals=0),
    )(own, ints)


UNROLL = 8


def spmm_kernel(plan, blocks, rand, out, acc):
    acc[...] = jnp.zeros_like(acc)
    size = acc.shape[0]
    per = out.shape[1] // size

    def pair(q):
        mats, rights = [], []
        for s in range(2):
            t = 2 * q + s
            code = plan[t // 128, lax.rem(t, 128)]
            k = jnp.maximum(lax.shift_right_logical(code, 16) - 1, 0)
            col = jnp.bitwise_and(code, 65535)
            mat = blocks[k]
            mats.append(jnp.where(code > 0, mat, jnp.zeros_like(mat)))
            rights.append(rand[col])
        return jnp.dot(
            jnp.concatenate(mats, axis=1),
            jnp.concatenate(rights, axis=0),
            preferred_element_type=F32,
        )

    def body(g, carry):
        prods = [pair(g * UNROLL + u) for u in range(UNROLL)]
        for u in range(UNROLL):
            q = g * UNROLL + u
            info = plan[4 + q // 128, lax.rem(q, 128)]
            keep = (1 - jnp.bitwise_and(info, 1)).astype(F32)
            value = acc[...] * keep + prods[u]
            acc[...] = value
            row = lax.shift_right_logical(info, 1)
            at = pl.multiple_of(lax.rem(row, per) * size, size)
            out[row // per, pl.ds(at, size), :] = value.astype(BF16)
        return carry

    lax.fori_loop(0, (plan[6, 0] + UNROLL - 1) // UNROLL, body, 0)


def spmm(plan, blocks, rand, leaves, leaf_rows):
    size, width = blocks.shape[1], rand.shape[2]
    return pl.pallas_call(
        spmm_kernel,
        name="spmm",
        out_shape=jax.ShapeDtypeStruct((leaves, leaf_rows, width), BF16),
        in_specs=[SMEM, VMEM, VMEM],
        out_specs=VMEM,
        scratch_shapes=[pltpu.VMEM((size, width), F32)],
        compiler_params=pltpu.CompilerParams(vmem_limit_bytes=4 << 20),
    )(plan, blocks, rand)


def dot_t(a, b):
    return lax.dot_general(a, b, (((1,), (1,)), ((), ())), preferred_element_type=F32)


def inverse_small(d):
    r = 1.0 / (d[0][0] * d[1][1] - d[0][1] * d[0][1])
    a00, a01, a11 = d[1][1] * r, -d[0][1] * r, d[0][0] * r
    x = [[a00 * d[0][2 + j] + a01 * d[1][2 + j] for j in range(2)], [a01 * d[0][2 + j] + a11 * d[1][2 + j] for j in range(2)]]
    s00 = d[2][2] - (d[0][2] * x[0][0] + d[1][2] * x[1][0])
    s01 = d[2][3] - (d[0][2] * x[0][1] + d[1][2] * x[1][1])
    s11 = d[3][3] - (d[0][3] * x[0][1] + d[1][3] * x[1][1])
    q = 1.0 / (s00 * s11 - s01 * s01)
    c00, c01, c11 = s11 * q, -s01 * q, s00 * q
    y = [[x[i][0] * c00 + x[i][1] * c01, x[i][0] * c01 + x[i][1] * c11] for i in range(2)]
    t00 = a00 + y[0][0] * x[0][0] + y[0][1] * x[0][1]
    t01 = a01 + y[0][0] * x[1][0] + y[0][1] * x[1][1]
    t11 = a11 + y[1][0] * x[1][0] + y[1][1] * x[1][1]
    return [
        [t00, t01, -y[0][0], -y[0][1]],
        [t01, t11, -y[1][0], -y[1][1]],
        [-y[0][0], -y[1][0], c00, c01],
        [-y[0][1], -y[1][1], c01, c11],
    ]


def inverse(a):
    n = a.shape[0]
    group, block = 8, 4
    lane = lax.broadcasted_iota(jnp.int32, (n, n), 1)
    sub = lax.broadcasted_iota(jnp.int32, (n, n), 0)
    lane1 = lax.broadcasted_iota(jnp.int32, (1, n), 1)

    def sweep(g, a):
        for k in range(0, group, block):
            span = range(block)
            d = [[None] * block for _ in span]
            for i in span:
                for j in range(i, block):
                    d[i][j] = jnp.broadcast_to(a[k + i : k + i + 1, k + j : k + j + 1], (1, n))
            inv = inverse_small(d)
            inside1 = (lane1 >= k) & (lane1 < k + block)
            right = [
                jnp.where(lane1 == k + j, -1.0, jnp.where(inside1, 0.0, a[k + j : k + j + 1, :])) for j in span
            ]
            insub = (sub >= k) & (sub < k + block)
            new = jnp.where(insub | ((lane >= k) & (lane < k + block)), 0.0, a)
            for i in span:
                row = inv[i][0] * right[0]
                for j in range(1, block):
                    row = row + inv[i][j] * right[j]
                col = jnp.broadcast_to(a[:, k + i : k + i + 1], (n, n))
                col = jnp.where(sub == k + i, -1.0, jnp.where(insub, 0.0, col))
                new = new - col * row
            a = new
        a = jnp.concatenate([a[group:], a[:group]], axis=0)
        return pltpu.roll(a, n - group, 1)

    return -lax.fori_loop(0, n // group, sweep, a)


def finish_kernel(
    perms, parent_perm, partial, basis, parent,
    mine, ksend, kin, sibling, wown, win, zout, zin, xout, xin, yout, yin, vout, vin, rzin, rxin,
    k_s, k_r, s_s, s_r, w_s, w_r, z_s, z_r, x_s, x_r, y_s, y_r, v_s, v_r, rz_s, rz_r, rx_s, rx_r,
):
    c = lax.axis_index("col")
    zh, x = c // 4, lax.rem(c, 4)
    leaf = partial.shape[1]
    peers = col_peers()
    n = len(peers)
    rank, width = mine.shape
    cut, raw = zout.shape[1], rzin.shape[1]
    top, last = leaf - 2 * raw, leaf - raw
    tile = 128

    barrier = pltpu.get_barrier_semaphore()
    for j in peers:
        pl.semaphore_signal(barrier, inc=1, device_id={"col": j}, device_id_type=MESH)

    def copy(src, dst, send_sem, recv_sem, j):
        return pltpu.make_async_remote_copy(
            src_ref=src, dst_ref=dst, send_sem=send_sem, recv_sem=recv_sem,
            device_id={"col": j}, device_id_type=MESH,
        )

    lanes = lax.broadcasted_iota(jnp.int32, (rank, leaf), 1)

    def down(row):
        return jnp.broadcast_to(row, (rank, rank)).T[:, :1]

    def pick(j):
        hot = jnp.where(lanes == down(perms[j, 0:1, :]), 1.0, 0.0).astype(BF16)
        return jnp.dot(hot, partial[j], preferred_element_type=F32)

    kc = []
    for i, j in enumerate(peers):
        ksend[i] = pick(j).astype(BF16)
        if i == 0:
            pl.semaphore_wait(barrier, n)
        cp = copy(ksend.at[i], kin.at[i], k_s.at[i], k_r.at[i], j)
        cp.start()
        kc.append(cp)
    total = pick(c)
    for cp in kc:
        cp.wait_recv()
    for i in range(n):
        total = total + kin[i].astype(F32)
    mine[...] = total.astype(BF16)
    to_sibling = copy(mine, sibling, s_s, s_r, c + 1 - 2 * lax.rem(c, 2))
    to_sibling.start()
    at_x = [lax.rem(x + d, 4) for d in range(4)]
    zpeer = (1 - zh) * 4 + x
    rz, rx = {}, {}
    for d in (2, 1, 3, 0):
        rz[d] = copy(
            partial.at[(1 - zh) * 4 + at_x[d], pl.ds(top, raw)], rzin.at[d], rz_s.at[d], rz_r.at[d], zpeer
        )
        rz[d].start()
        if d == 0:
            continue
        for h in range(2):
            rx[d, h] = copy(
                partial.at[lax.rem(zh + h, 2) * 4 + at_x[d], pl.ds(last, raw)],
                rxin.at[d - 1, h], rx_s.at[d - 1, h], rx_r.at[d - 1, h], zh * 4 + at_x[d],
            )
            rx[d, h].start()

    skel = mine[...]
    wown[...] = jnp.dot(
        inverse(dot_t(skel, skel)), skel.astype(F32), precision=HI, preferred_element_type=F32
    ).astype(BF16)
    wc = []
    for i, j in enumerate(peers):
        cp = copy(wown, win.at[i], w_s.at[i], w_r.at[i], j)
        cp.start()
        wc.append(cp)

    def times(j, first, last, weight, put):
        value = dot_t(partial[j, pl.ds(first, last - first), :], weight[...])
        put(pl.ds(0, last - first), value)

    def store(ref):
        def put(at, value):
            ref[at, :] = value.astype(ref.dtype)

        return put

    times(c, 0, top, wown, store(basis))

    piece = {o: OFFSETS.index(((2 - o[0]) % 2, (4 - o[1]) % 4)) for o in OFFSETS}
    zc, xc = {}, {}
    for d in (2, 1, 3, 0):
        wc[piece[(1, d)]].wait_recv()
        weight = win.at[piece[(1, d)]]
        j = (1 - zh) * 4 + at_x[d]
        times(j, 0, cut, weight, store(zout.at[d]))
        zc[d] = copy(zout.at[d], zin.at[d], z_s.at[d], z_r.at[d], zpeer)
        zc[d].start()
        if d == 0:
            continue
        times(j, cut, top, weight, store(xout.at[d - 1, 1]))
        xc[d, 1] = copy(xout.at[d - 1, 1], xin.at[d - 1, 1], x_s.at[d - 1, 1], x_r.at[d - 1, 1], zh * 4 + at_x[d])
        xc[d, 1].start()
        wc[piece[(0, d)]].wait_recv()
        times(zh * 4 + at_x[d], cut, top, win.at[piece[(0, d)]], store(xout.at[d - 1, 0]))
        xc[d, 0] = copy(xout.at[d - 1, 0], xin.at[d - 1, 0], x_s.at[d - 1, 0], x_r.at[d - 1, 0], zh * 4 + at_x[d])
        xc[d, 0].start()

    to_sibling.wait()
    odd = lax.rem(c, 2)
    other = sibling[...]
    both = jnp.concatenate([jnp.where(odd == 0, skel, other), jnp.where(odd == 0, other, skel)], axis=0)
    lanes2 = lax.broadcasted_iota(jnp.int32, (rank, 2 * rank), 1)
    order = parent_perm[pl.ds((lax.axis_index("row") * (n + 1) + c) // 2, 1), :]
    hot = jnp.where(lanes2 == down(order[:, :rank]), 1.0, 0.0).astype(BF16)
    chosen = jnp.dot(hot, both, preferred_element_type=F32).astype(BF16)
    parent[...] = jnp.dot(
        dot_t(skel, chosen), inverse(dot_t(chosen, chosen)), precision=HI, preferred_element_type=F32
    )

    def over_z(d):
        rz[d].wait_recv()
        return (partial[zh * 4 + at_x[d], pl.ds(top, raw), :].astype(F32) + rzin[d].astype(F32)).astype(BF16)

    def over_x(h):
        for e in (2, 1, 3):
            rx[e, h].wait_recv()
        value = partial[lax.rem(zh + h, 2) * 4 + x, pl.ds(last, raw), :].astype(F32)
        for e in range(3):
            value = value + rxin[e, h].astype(F32)
        return value.astype(BF16)

    yc = {}
    for d in (2, 1, 3):
        zc[d].wait_recv()

        def put(at, value, d=d):
            yout[d - 1, at, :] = (value + zin[d, at, :].astype(F32)).astype(BF16)

        times(zh * 4 + at_x[d], 0, cut, win.at[piece[(0, d)]], put)
        yout[d - 1, pl.ds(cut, raw), :] = dot_t(over_z(d), win[piece[(0, d)]]).astype(BF16)
        yc[d] = copy(yout.at[d - 1], yin.at[d - 1], y_s.at[d - 1], y_r.at[d - 1], zh * 4 + at_x[d])
        yc[d].start()
        if d == 1:
            for e in (2, 1, 3):
                xc[e, 1].wait_recv()

            def put_v(at, value):
                for e in range(3):
                    value = value + xin[e, 1, at, :].astype(F32)
                vout[at, :] = value.astype(BF16)

            times(zpeer, cut, top, win.at[piece[(1, 0)]], put_v)
            vout[pl.ds(top - cut, raw), :] = dot_t(over_x(1), win[piece[(1, 0)]]).astype(BF16)
            vc = copy(vout, vin, v_s, v_r, zpeer)
            vc.start()

    basis[pl.ds(top, raw), :] = dot_t(over_z(0), wown[...])
    basis[pl.ds(last, raw), :] = dot_t(over_x(0), wown[...])
    for e in (2, 1, 3):
        xc[e, 0].wait_recv()
    zc[0].wait_recv()
    vc.wait_recv()

    def add_high(t, carry):
        at = pl.multiple_of(t * tile, tile)
        value = basis[pl.ds(cut + at, tile), :] + vin[pl.ds(at, tile), :].astype(F32)
        for e in range(3):
            value = value + xin[e, 0, pl.ds(at, tile), :].astype(F32)
        basis[pl.ds(cut + at, tile), :] = value
        return carry

    lax.fori_loop(0, (top - cut) // tile, add_high, 0)
    basis[pl.ds(last, raw), :] = basis[pl.ds(last, raw), :] + vin[pl.ds(top - cut, raw), :].astype(F32)
    for d in (2, 1, 3):
        yc[d].wait_recv()

    def add_low(t, carry):
        at = pl.ds(pl.multiple_of(t * tile, tile), tile)
        value = basis[at, :] + zin[0, at, :].astype(F32)
        for e in range(3):
            value = value + yin[e, at, :].astype(F32)
        basis[at, :] = value
        return carry

    lax.fori_loop(0, cut // tile, add_low, 0)
    value = basis[pl.ds(top, raw), :]
    for e in range(3):
        value = value + yin[e, pl.ds(cut, raw), :].astype(F32)
    basis[pl.ds(top, raw), :] = value
    for cp in kc + wc + list(zc.values()) + list(xc.values()) + list(yc.values()) + list(rz.values()) + list(rx.values()) + [vc]:
        cp.wait_send()


def finish(perms, parent_perm, partial):
    count, _, rank = perms.shape
    leaf, width = partial.shape[1:]
    n = count - 1
    raw = leaf // 16
    cut = leaf * 9 // 16
    dma = pltpu.SemaphoreType.DMA
    return pl.pallas_call(
        finish_kernel,
        name="finish",
        out_shape=(
            jax.ShapeDtypeStruct((leaf, rank), F32),
            jax.ShapeDtypeStruct((rank, rank), F32),
        ),
        in_specs=[VMEM, VMEM, VMEM],
        out_specs=(VMEM, VMEM),
        scratch_shapes=[
            pltpu.VMEM((rank, width), BF16),
            pltpu.VMEM((n, rank, width), BF16),
            pltpu.VMEM((n, rank, width), BF16),
            pltpu.VMEM((rank, width), BF16),
            pltpu.VMEM((rank, width), BF16),
            pltpu.VMEM((n, rank, width), BF16),
            pltpu.VMEM((4, cut, rank), BF16),
            pltpu.VMEM((4, cut, rank), BF16),
            pltpu.VMEM((3, 2, leaf - cut - 2 * raw, rank), BF16),
            pltpu.VMEM((3, 2, leaf - cut - 2 * raw, rank), BF16),
            pltpu.VMEM((3, cut + raw, rank), BF16),
            pltpu.VMEM((3, cut + raw, rank), BF16),
            pltpu.VMEM((leaf - cut - raw, rank), BF16),
            pltpu.VMEM((leaf - cut - raw, rank), BF16),
            pltpu.VMEM((4, raw, width), BF16),
            pltpu.VMEM((3, 2, raw, width), BF16),
            dma((n,)), dma((n,)), dma, dma, dma((n,)), dma((n,)),
            dma((4,)), dma((4,)), dma((3, 2)), dma((3, 2)), dma((3,)), dma((3,)), dma, dma,
            dma((4,)), dma((4,)), dma((3, 2)), dma((3, 2)),
        ],
        compiler_params=pltpu.CompilerParams(
            collective_id=1, has_side_effects=True, vmem_limit_bytes=24 << 20
        ),
    )(perms, parent_perm, partial)


def deliver_kernel(basis, parent, basis_out, parent_out, sems):
    first = pltpu.make_async_copy(basis, basis_out, sems.at[0])
    second = pltpu.make_async_copy(parent, parent_out, sems.at[1])
    first.start()
    second.start()
    first.wait()
    second.wait()


def deliver(basis, parent):
    return pl.pallas_call(
        deliver_kernel,
        name="deliver",
        out_shape=(
            jax.ShapeDtypeStruct(basis.shape, basis.dtype),
            jax.ShapeDtypeStruct(parent.shape, parent.dtype),
        ),
        in_specs=[VMEM, VMEM],
        out_specs=(HBM, HBM),
        scratch_shapes=[pltpu.SemaphoreType.DMA((2,))],
        compiler_params=pltpu.CompilerParams(vmem_limit_bytes=4 << 20),
    )(basis, parent)


def local(blocks, block_row, block_col, random_cols, leaf_perm, parent_perm):
    n_col = lax.axis_size("col")
    leaf_rows, width = random_cols.shape[2:]
    size = blocks.shape[1]
    rank = parent_perm.shape[1] // 2
    gathered, perms, plan = gather(
        random_cols.reshape(leaf_rows, width), block_row, block_col, leaf_perm.reshape(-1), rank
    )
    partial_value = spmm(plan, blocks, gathered.reshape(-1, size, width), n_col, leaf_rows)
    return deliver(*finish(perms, parent_perm, partial_value))


def solution(mesh):
    in_specs = (
        P(("row", "col"), None, None),
        P(("row", "col")),
        P(("row", "col")),
        P("col", "row", None, None),
        P(("row", "col"), None),
        P(),
    )
    out_specs = (P(("row", "col"), None), P(("row", "col"), None))
    return jax.shard_map(local, mesh=mesh, in_specs=in_specs, out_specs=out_specs, check_vma=False)
```
